32 devices in a mesh: groups: 2 (over x), ctx: 16 (over z, y, core).
Axes of the slice: x: 2, y: 2, z: 4, core: 2. Of those that a mesh axis runs over, the one named last changes fastest.
Arguments:
- queries: bfloat16 [96, 4096], P(('groups', 'ctx')), parts along dimension 0, may hold values from -200 to 200
- cache_keys: bfloat16 [4096, 512], P(('groups', 'ctx')), parts along dimension 0, may hold values from -6 to 6
- cache_values: bfloat16 [4096, 512], P(('groups', 'ctx')), parts along dimension 0, may hold values from -6 to 6
- new_keys: bfloat16 [96, 512], P(('groups', 'ctx')), parts along dimension 0, may hold values from -6 to 6
- new_values: bfloat16 [96, 512], P(('groups', 'ctx')), parts along dimension 0, may hold values from -6 to 6
- cache_lengths: int32 [32], P(('groups', 'ctx')), parts along dimension 0, may hold values from 0 to 128, as said below
- residual_in: bfloat16 [96, 2048], P(('groups', 'ctx')), parts along dimension 0, may hold values from -6 to 6
- out_weight: bfloat16 [4096, 2048], P('ctx'), may hold values from -3 to 3
- norm_gain: bfloat16 [2048], replicated, may hold values from 0.25 to 1.75
- expert_gate: bfloat16 [16, 2048, 768], P('ctx'), may hold values from -0.125 to 0.125
- expert_up: bfloat16 [16, 2048, 768], P('ctx'), may hold values from -0.125 to 0.125
- expert_down: bfloat16 [16, 768, 2048], P('ctx'), may hold values from -0.21875 to 0.21875
- expert_ids: int32 [96, 8], P(('groups', 'ctx')), parts along dimension 0, may hold values from 0 to 15, all different within a row; in each aligned block of 3 rows (0 to 2, 3 to 5, ...) at most 3 rows name the same one
- expert_weights: float32 [96, 8], P(('groups', 'ctx')), parts along dimension 0, may hold values from 0.03 to 0.4
Outputs:
- layer_out: bfloat16 [96, 2048], P(('groups', 'ctx')), parts along dimension 0
The draws below stay inside these ranges and needn't reach their ends.
There are 2 independent parts, one for each index of `groups`. The reference program is written for one: setup_inputs(seed, part) draws one part's arguments, and reference() takes and returns one part's arrays. A program takes and returns all parts, laid end to end along the dimension named above; an argument that names none is the same for every part. Nothing has to cross between parts.
Inputs may be any that keep to these rules, and one draw needn't show every extreme that they name: `cache_lengths`: some shard in every draw is full, with 128 live positions. `expert_ids`: within one block of 3 rows no expert is named more than 3 times, a bound that some block reaches.
All inputs are finite; a program needn't handle non-finite values.
Results may differ from the reference program's by a relative error of at most 0.01.
Values may be sent and summed in bfloat16 or wider, within the bound.
A program may use at most 64 MiB of HBM per device.

```python
import math
import jax
import jax.numpy as jnp
import numpy as np
from jax import lax

D = 2048
HEADS = 32
KV_HEADS = 4
HEAD_DIM = 128
FF = 768
TOP = 8
C_DEV = 128
ROWS_DEV = 3
CAP = 3
SHARDS = 16
EXPERTS = 16
ROWS = 48
CACHE = 2048
WQ = 4096
KVW = 512


def shard_lengths(key):
    first, second = jax.random.split(jax.random.fold_in(key, 11))
    base = jax.random.randint(first, (SHARDS,), 0, C_DEV // 2 + 1)
    chosen = jax.random.randint(second, (), 0, SHARDS)
    lengths = jnp.where(jnp.arange(SHARDS) == chosen, C_DEV, base)
    return lengths.astype(jnp.int32)


def cache_rows(key):
    rows_f = jax.random.truncated_normal(jax.random.fold_in(key, 23), -6.0, 6.0, (CACHE, KV_HEADS, HEAD_DIM), jnp.float32)
    return rows_f


def draw_cache_lengths(key, part):
    return shard_lengths(key)


def draw_cache_keys(key, part):
    return cache_rows(key).reshape(CACHE, KV_HEADS * HEAD_DIM).astype(jnp.bfloat16)


def draw_queries(key, part):
    draws = jax.random.truncated_normal(jax.random.fold_in(key, 37), -6.0, 6.0, (ROWS, HEADS, HEAD_DIM), jnp.float32)
    return draws.reshape(ROWS, HEADS * HEAD_DIM).astype(jnp.bfloat16)


def block_scale(stream_key, extent, shards, low, largest):
    level, own = 1.0, jax.random.fold_in(stream_key, 6)
    for axis_at, parts in shards:
        heights = jnp.exp(jax.random.uniform(jax.random.fold_in(own, axis_at), (parts,), jnp.float32, low / len(shards), largest / len(shards)))
        level = level * jnp.repeat(heights, extent[axis_at] // parts).reshape([-1 if axis == axis_at else 1 for axis in range(len(extent))])
    return level


def assign_block(stream_key, own, number, rows, amount, top, reach, lean):
    sequence = jax.random.permutation(stream_key, amount)
    packed, ordinary = shares(amount, rows * top, reach, lean, True), shares(amount, rows * top, reach, lean, False)
    places = jnp.arange(amount)

    def named(sizes, rotation):
        used = int((sizes > 0).sum())
        fixed = max(1, used // 4)
        moved = fixed + (places - fixed + rotation * (used - fixed)) % max(1, amount - fixed)
        return jnp.zeros((amount,), jnp.int32).at[sequence[jnp.where(places < fixed, places, moved)]].set(jnp.asarray(sizes, jnp.int32))

    sizes = jnp.where(number % 4 == 0, named(packed, number // 4), named(ordinary, number - number // 4 - 1))
    mixed = jax.random.permutation(jax.random.fold_in(own, 3), amount)
    source_of, receiver = mixed[0:amount // 2 * 2:2], mixed[1:amount // 2 * 2:2]
    margin = jnp.minimum(sizes[source_of] - 1, reach - sizes[receiver]) // 2
    margin = jnp.where((source_of == sequence[0]) | (receiver == sequence[0]) | (sizes[receiver] == 0), 0, jnp.maximum(margin, 0))
    moved = jax.random.randint(jax.random.fold_in(own, 4), (amount // 2,), 0, 1 << 20) % (margin + 1)
    sizes = sizes.at[source_of].add(-moved).at[receiver].add(moved)
    items = jnp.searchsorted(jnp.cumsum(sizes), jnp.arange(rows * top), side="right").astype(jnp.int32)
    table = items.reshape(top, rows).T
    table = table[jax.random.permutation(jax.random.fold_in(own, 1), rows)]
    rotation = jax.random.randint(jax.random.fold_in(own, 2), (rows, 1), 0, top)
    return jnp.take_along_axis(table, (jnp.arange(top)[None, :] + rotation) % top, axis=1)


def shares(number_of, total, reach, lean, full):
    weights = [(1 << 20) // math.isqrt(rank ** lean) + 1 for rank in range(1, number_of + 1)]
    largest = reach if full else min(reach, max(-(-total // number_of), total * weights[0] // sum(weights)))
    least = 1 if total - largest >= number_of - 1 else 0
    given, rest = [largest] + [least] * (number_of - 1), total - largest - least * (number_of - 1)
    while rest > 0:
        movable = [i for i in range(1, number_of) if given[i] < largest] or [i for i in range(1, number_of) if given[i] < reach]
        whole, remaining = sum([weights[i] for i in movable]), rest
        for i in movable:
            more = min(reach - given[i], max(1, remaining * weights[i] // whole), rest)
            given[i] = given[i] + more
            rest = rest - more
    return np.array(given)


def bell_draw(own_key, extent, spread, reach, pieces=(), held_as=jnp.bfloat16):
    values = spread * jax.random.normal(own_key, extent, jnp.float32)
    if pieces:
        values = values * block_scale(own_key, extent, pieces, -0.22, 0.18)
    return jnp.clip(values, -reach, reach).astype(held_as)


def setup_inputs(seed: int = 0, part: int = 0) -> dict:
    key_of = jax.random.split(jax.random.key(seed), 15)
    part_splits = jax.random.split(jax.random.fold_in(key_of[14], part), 15)
    queries = draw_queries(jax.random.fold_in(jax.random.fold_in(key_of[14], part), 71), part)
    cache_keys = draw_cache_keys(jax.random.fold_in(jax.random.fold_in(key_of[14], part), 71), part)
    cache_values = bell_draw(part_splits[2], (CACHE, KVW), 1.0, 6.0, ((0, 16),))
    new_keys = bell_draw(part_splits[3], (ROWS, KVW), 1.0, 6.0, ((0, 16),))
    new_values = bell_draw(part_splits[4], (ROWS, KVW), 1.0, 6.0, ((0, 16),))
    cache_lengths = draw_cache_lengths(jax.random.fold_in(jax.random.fold_in(key_of[14], part), 71), part)
    residual_in = bell_draw(part_splits[6], (ROWS, D), 1.0, 6.0, ((0, 16),))
    out_weight = bell_draw(key_of[7], (WQ, D), 0.5, 3.0, ((0, 16),))
    norm_gain = jnp.clip(1.0 + 0.15 * jax.random.normal(key_of[8], (D,), jnp.float32), 0.25, 1.75).astype(jnp.bfloat16)
    expert_gate = bell_draw(key_of[9], (EXPERTS, D, FF), D ** -0.5, 0.125, ((0, 16),))
    expert_up = bell_draw(key_of[10], (EXPERTS, D, FF), D ** -0.5, 0.125, ((0, 16),))
    expert_down = bell_draw(key_of[11], (EXPERTS, FF, D), FF ** -0.5, 0.21875, ((0, 16),))
    expert_ids_keys = jax.random.split(jax.random.fold_in(part_splits[12], 1), ROWS // ROWS_DEV)
    expert_ids_turns = jax.random.permutation(jax.random.fold_in(part_splits[12], 3), ROWS // ROWS_DEV)
    expert_ids = jax.vmap(lambda own, number: assign_block(jax.random.fold_in(part_splits[12], 2), own, number, ROWS_DEV, EXPERTS, TOP, CAP, 2))(expert_ids_keys, expert_ids_turns).reshape((ROWS, TOP))
    expert_weights = jnp.clip(jnp.exp(math.log(0.4) - 2.5902672 * jax.random.uniform(part_splits[13], (ROWS, TOP), jnp.float32) ** block_scale(part_splits[13], (ROWS, TOP), ((0, 16),), -0.2, 0.2)), 0.03, 0.4)
    return {"queries": queries, "cache_keys": cache_keys, "cache_values": cache_values, "new_keys": new_keys, "new_values": new_values, "cache_lengths": cache_lengths, "residual_in": residual_in, "out_weight": out_weight, "norm_gain": norm_gain, "expert_gate": expert_gate, "expert_up": expert_up, "expert_down": expert_down, "expert_ids": expert_ids, "expert_weights": expert_weights}


MASKED = -1e+30
epsilon = 1e-06

def slot_numbers(block_ids):
    flat_ids = block_ids.reshape(-1)
    count = flat_ids.shape[0]
    places = jnp.arange(count, dtype=jnp.int32)
    earlier = (flat_ids[:, None] == flat_ids[None, :]) & (places[None, :] < places[:, None])
    ranks = lax.optimization_barrier(jnp.sum(earlier.astype(jnp.int32), axis=1))
    return (flat_ids * CAP + ranks).astype(jnp.int32)

def reference(queries, cache_keys, cache_values, new_keys, new_values, cache_lengths, residual_in, out_weight, norm_gain, expert_gate, expert_up, expert_down, expert_ids, expert_weights):
    group_size = HEADS // KV_HEADS
    query_heads = queries.reshape(ROWS, HEADS, HEAD_DIM)
    key_rows = jnp.concatenate([cache_keys, new_keys], 0).reshape(CACHE + ROWS, KV_HEADS, HEAD_DIM)
    value_rows = jnp.concatenate([cache_values, new_values], 0).reshape(CACHE + ROWS, KV_HEADS, HEAD_DIM)
    positions = jnp.arange(CACHE, dtype=jnp.int32)
    cache_ok = positions % C_DEV < cache_lengths[positions // C_DEV]
    row_ids = jnp.arange(ROWS, dtype=jnp.int32)
    span_ok = row_ids[None, :] <= row_ids[:, None]
    usable = jnp.concatenate([jnp.broadcast_to(cache_ok[None, :], (ROWS, CACHE)), span_ok], 1)

    def single_head(head):
        query_one = lax.dynamic_index_in_dim(query_heads, head, 1, False)
        key_one = lax.dynamic_index_in_dim(key_rows, head // group_size, 1, False)
        value_one = lax.dynamic_index_in_dim(value_rows, head // group_size, 1, False)
        scores = jnp.dot(query_one, key_one.T, preferred_element_type=jnp.float32) * HEAD_DIM ** (-0.5)
        scores = jnp.where(usable, scores, MASKED)
        maxima = lax.optimization_barrier(jnp.max(scores, axis=1, keepdims=True))
        exp_weights = jnp.where(usable, jnp.exp(scores - maxima), 0.0)
        totals = lax.optimization_barrier(jnp.sum(exp_weights, axis=1, keepdims=True))
        summed = jnp.dot(exp_weights.astype(jnp.bfloat16), value_one, preferred_element_type=jnp.float32)
        return summed / totals
    heads_out = lax.map(single_head, jnp.arange(HEADS, dtype=jnp.int32))
    attention = heads_out.transpose(1, 0, 2).reshape(ROWS, WQ).astype(jnp.bfloat16)
    projected = jnp.dot(attention, out_weight, preferred_element_type=jnp.float32)
    state = residual_in.astype(jnp.float32) + projected
    normed = (state * lax.rsqrt(lax.optimization_barrier(jnp.mean(state * state, axis=1, keepdims=True)) + epsilon) * norm_gain.astype(jnp.float32)).astype(jnp.bfloat16)
    n_slots = EXPERTS * CAP
    slot_of = jax.vmap(slot_numbers)(expert_ids.reshape(SHARDS, ROWS_DEV, TOP))
    one_hot = (slot_of[:, :, None] == jnp.arange(n_slots, dtype=jnp.int32)[None, None, :]).astype(jnp.float32)
    dispatch_map = one_hot.reshape(SHARDS, ROWS_DEV, TOP, n_slots).sum(2)
    normed_blocks = normed.reshape(SHARDS, ROWS_DEV, D).astype(jnp.float32)
    outgoing = jnp.einsum('srn,srd->snd', dispatch_map, normed_blocks, precision=lax.Precision.HIGHEST).astype(jnp.bfloat16)
    outgoing = outgoing.reshape(SHARDS, EXPERTS, CAP, D).transpose(1, 0, 2, 3)

    def expert_work(inputs):
        received, gate_w, up_w, down_w = inputs
        flat_rows = received.reshape(SHARDS * CAP, D)
        gate_out = jnp.dot(flat_rows, gate_w, preferred_element_type=jnp.float32)
        up_out = jnp.dot(flat_rows, up_w, preferred_element_type=jnp.float32)
        activated = (jax.nn.silu(gate_out) * up_out).astype(jnp.bfloat16)
        expert_out = jnp.dot(activated, down_w, preferred_element_type=jnp.float32).astype(jnp.bfloat16)
        return expert_out.reshape(SHARDS, CAP, D)
    results = lax.map(expert_work, (outgoing, expert_gate, expert_up, expert_down))
    back = results.transpose(1, 0, 2, 3).reshape(SHARDS, n_slots, D)
    combine_map = (one_hot * expert_weights.reshape(SHARDS, ROWS_DEV * TOP)[:, :, None]).reshape(SHARDS, ROWS_DEV, TOP, n_slots).sum(2)
    expert_sum = jnp.einsum('srn,snd->srd', combine_map, back.astype(jnp.float32), precision=lax.Precision.HIGHEST).reshape(ROWS, D)
    return (state + expert_sum).astype(jnp.bfloat16)
```

```python
import functools

import jax
import jax.numpy as jnp
from jax import lax
from jax.experimental import pallas as pl
from jax.experimental.pallas import tpu as pltpu
from jax.sharding import PartitionSpec as P

HEADS = 32
KV_HEADS = 4
HEAD_DIM = 128
TOP = 8


MASKED = -1e30
epsilon = 1e-06


def plain(
    queries,
    cache_keys,
    cache_values,
    new_keys,
    new_values,
    cache_lengths,
    residual_in,
    out_weight,
    norm_gain,
    expert_gate,
    expert_up,
    expert_down,
    expert_ids,
    expert_weights,
):
    shards = lax.axis_size("ctx")
    device = lax.axis_index("ctx")
    rows_dev = residual_in.shape[0]
    capacity = max(2, 2 * rows_dev * TOP // shards)
    group_size = HEADS // KV_HEADS
    whole_queries = lax.all_gather(queries, "ctx", axis=0, tiled=True)
    all_rows = whole_queries.shape[0]
    query_heads = whole_queries.reshape(all_rows, KV_HEADS, group_size, HEAD_DIM)
    local_cache = cache_keys.shape[0]
    key_rows = jnp.concatenate([cache_keys, new_keys], 0).reshape(
        local_cache + rows_dev, KV_HEADS, HEAD_DIM
    )
    value_rows = jnp.concatenate([cache_values, new_values], 0).reshape(
        local_cache + rows_dev, KV_HEADS, HEAD_DIM
    )
    slot_ids = jnp.arange(local_cache + rows_dev, dtype=jnp.int32)
    span_pos = device * rows_dev + slot_ids - local_cache
    row_ids = jnp.arange(all_rows, dtype=jnp.int32)
    usable = jnp.where(
        slot_ids[None, :] < local_cache,
        (slot_ids < cache_lengths[0])[None, :],
        span_pos[None, :] <= row_ids[:, None],
    )
    scores = jnp.einsum(
        "rkgd,nkd->kgrn", query_heads, key_rows, preferred_element_type=jnp.float32
    ) * HEAD_DIM ** (-0.5)
    scores = jnp.where(usable, scores, MASKED)
    maxima = jnp.max(scores, axis=-1)
    exp_weights = jnp.where(usable, jnp.exp(scores - maxima[..., None]), 0.0)
    totals = jnp.sum(exp_weights, axis=-1)
    numerators = jnp.einsum(
        "kgrn,nkd->rkgd",
        exp_weights.astype(jnp.bfloat16),
        value_rows,
        preferred_element_type=jnp.float32,
    ).reshape(all_rows, HEADS, HEAD_DIM)
    maxima = maxima.transpose(2, 0, 1).reshape(all_rows, HEADS)
    totals = totals.transpose(2, 0, 1).reshape(all_rows, HEADS)
    largest = lax.pmax(maxima, "ctx")
    rescale = jnp.exp(maxima - largest)
    denoms = lax.psum(totals * rescale, "ctx")
    weighted = (numerators * (rescale / denoms)[..., None]).reshape(all_rows, HEADS * HEAD_DIM)
    columns = lax.psum_scatter(weighted, "ctx", scatter_dimension=1, tiled=True).astype(
        jnp.bfloat16
    )
    projected = lax.psum_scatter(
        jnp.dot(columns, out_weight, preferred_element_type=jnp.float32),
        "ctx",
        scatter_dimension=0,
        tiled=True,
    )
    state = residual_in.astype(jnp.float32) + projected
    normed = (
        state
        * lax.rsqrt(jnp.mean(state * state, axis=1, keepdims=True) + epsilon)
        * norm_gain.astype(jnp.float32)
    ).astype(jnp.bfloat16)
    n_slots = shards * capacity
    flat_ids = expert_ids.reshape(-1)
    places = jnp.arange(flat_ids.shape[0], dtype=jnp.int32)
    earlier = (flat_ids[:, None] == flat_ids[None, :]) & (places[None, :] < places[:, None])
    slot_of = flat_ids * capacity + jnp.sum(earlier.astype(jnp.int32), axis=1)
    one_hot = (slot_of[:, None] == jnp.arange(n_slots, dtype=jnp.int32)[None, :]).astype(
        jnp.float32
    )
    dispatch_map = one_hot.reshape(rows_dev, TOP, n_slots).sum(1)
    outgoing = (
        jnp.dot(dispatch_map.T.astype(jnp.bfloat16), normed, preferred_element_type=jnp.float32)
        .astype(jnp.bfloat16)
        .reshape(shards, capacity, normed.shape[1])
    )
    received = lax.all_to_all(outgoing, "ctx", split_axis=0, concat_axis=0, tiled=True)
    gate_out = jnp.einsum(
        "scd,df->scf", received, expert_gate[0], preferred_element_type=jnp.float32
    )
    up_out = jnp.einsum("scd,df->scf", received, expert_up[0], preferred_element_type=jnp.float32)
    activated = (jax.nn.silu(gate_out) * up_out).astype(jnp.bfloat16)
    expert_out = jnp.einsum(
        "scf,fd->scd", activated, expert_down[0], preferred_element_type=jnp.float32
    ).astype(jnp.bfloat16)
    back = lax.all_to_all(expert_out, "ctx", split_axis=0, concat_axis=0, tiled=True)
    combine_map = (
        (one_hot * expert_weights.reshape(-1)[:, None]).reshape(rows_dev, TOP, n_slots).sum(1)
    )
    expert_sum = jnp.dot(
        combine_map,
        back.reshape(n_slots, normed.shape[1]).astype(jnp.float32),
        precision=lax.Precision.HIGHEST,
    )
    return (state + expert_sum).astype(jnp.bfloat16)


LANES = 128
SUB = 8
HALF = SUB // 2
MESH = pl.DeviceIdType.MESH
F32 = jnp.float32
BF16 = jnp.bfloat16
Q, K, V, NEW, NUM, STAT, PROJ, ROWS, BACK = range(9)


def fits(shards, rows_dev, width, capacity, experts_dev):
    team = shards // KV_HEADS
    if shards % KV_HEADS or team == 0 or (HEADS // KV_HEADS) % team:
        return False
    pair = HEADS // KV_HEADS // team
    return (
        experts_dev == 1
        and HEAD_DIM == LANES
        and shards * SUB == LANES
        and rows_dev < HALF
        and pair * rows_dev <= SUB
        and capacity >= rows_dev
        and width % (4 * LANES) == 0
    )


def layer_kernel(
    shards,
    q_ref,
    ck_ref,
    cv_ref,
    nk_ref,
    nv_ref,
    len_ref,
    res_ref,
    wo_ref,
    gain_ref,
    wg_ref,
    wu_ref,
    wd_ref,
    ids_ref,
    ew_ref,
    out_ref,
    wo,
    wg,
    wu,
    wd,
    q_wide,
    q_send,
    q_recv,
    q_heads,
    k_all,
    v_all,
    new_wide,
    new_send,
    new_recv,
    num_send,
    num_recv,
    stat_send,
    stat_recv,
    proj_send,
    proj_recv,
    res_wide,
    gain_wide,
    ids_wide,
    ew_wide,
    mix,
    row_send,
    row_recv,
    x_all,
    act,
    back_send,
    back_recv,
    load_sem,
    send_sem,
    recv_sem,
):
    me = lax.axis_index("ctx")
    team = shards // KV_HEADS
    pair = HEADS // KV_HEADS // team
    rows_dev, width = res_ref.shape
    chunks = width // LANES
    cache = ck_ref.shape[0]
    head, mate = me // team, me % team

    barrier = pltpu.get_barrier_semaphore()

    def greet(step, carry):
        pl.semaphore_signal(
            barrier, inc=1, device_id={"ctx": lax.rem(me + step, shards)}, device_id_type=MESH
        )
        return carry

    lax.fori_loop(1, shards, greet, 0)

    own_lanes = pl.ds(pl.multiple_of(head * LANES, LANES), LANES)
    loads = [
        pltpu.make_async_copy(ck_ref.at[:, own_lanes], k_all.at[head], load_sem.at[0]),
        pltpu.make_async_copy(cv_ref.at[:, own_lanes], v_all.at[head], load_sem.at[1]),
        pltpu.make_async_copy(wo_ref, wo, load_sem.at[2]),
        pltpu.make_async_copy(wg_ref.at[0], wg, load_sem.at[3]),
        pltpu.make_async_copy(wu_ref.at[0], wu, load_sem.at[4]),
        pltpu.make_async_copy(wd_ref.at[0], wd, load_sem.at[5]),
    ]
    for load in loads:
        load.start()

    q_wide[...] = jnp.zeros_like(q_wide)
    for one in range(HEADS):
        kv, rest = divmod(one, HEADS // KV_HEADS)
        who, which = divmod(rest, pair)
        q_wide[kv, pl.ds(who * SUB + which * rows_dev, rows_dev), :] = q_ref[
            :, one * LANES : (one + 1) * LANES
        ].astype(F32)
    q_send[...] = q_wide[...].astype(BF16)
    new_wide[...] = jnp.zeros_like(new_wide)
    live = jnp.full((1, LANES), len_ref[0], jnp.int32).astype(F32)
    for kv in range(KV_HEADS):
        lanes = slice(kv * LANES, (kv + 1) * LANES)
        new_wide[kv, 0:rows_dev, :] = nk_ref[:, lanes].astype(F32)
        new_wide[kv, rows_dev : rows_dev + 1, :] = live
        new_wide[kv, SUB : SUB + rows_dev, :] = nv_ref[:, lanes].astype(F32)
    new_send[...] = new_wide[...].astype(BF16)

    def remote(kind, src, dst, target, source):
        return pltpu.make_async_remote_copy(
            src_ref=src,
            dst_ref=dst,
            send_sem=send_sem.at[kind, target],
            recv_sem=recv_sem.at[kind, source],
            device_id={"ctx": target},
            device_id_type=MESH,
        )

    def column(step):
        other = lax.rem(head + step, KV_HEADS)
        return other, other * team + mate

    def key_copies(other, target, source_head):
        lanes = pl.ds(pl.multiple_of(other * LANES, LANES), LANES)
        source = source_head * team + mate
        return (
            remote(K, ck_ref.at[:, lanes], k_all.at[source_head], target, source),
            remote(V, cv_ref.at[:, lanes], v_all.at[source_head], target, source),
            remote(NEW, new_send.at[other], new_recv.at[source_head], target, source),
        )

    pl.semaphore_wait(barrier, shards - 1)

    def peers(body):
        def step_body(step, carry):
            body(lax.rem(me + step, shards))
            return carry

        lax.fori_loop(1, shards, step_body, 0)

    def q_copy(target, source):
        return remote(Q, q_send.at[target // team], q_recv.at[source], target, source)

    for step in range(1, KV_HEADS):
        for copy in key_copies(*column(step), head):
            copy.start()
    peers(lambda other: q_copy(other, me).start())

    q_recv[me] = q_send[head]
    new_recv[head] = new_send[head]

    res_wide[...] = jnp.zeros_like(res_wide)
    for c in range(chunks):
        lanes = slice(c * LANES, (c + 1) * LANES)
        res_wide[c * HALF : c * HALF + rows_dev, :] = res_ref[:, lanes].astype(F32)
        gain_wide[c * HALF : (c + 1) * HALF, :] = jnp.broadcast_to(
            gain_ref[:, lanes].astype(F32), (HALF, LANES)
        )
    ids_wide[...] = jnp.full_like(ids_wide, -1)
    ew_wide[...] = jnp.zeros_like(ew_wide)
    for half in range(2):
        at = slice(half * HALF, half * HALF + rows_dev)
        ids_wide[at, :] = ids_ref[...]
        ew_wide[at, :] = ew_ref[...]
    for e in range(shards):
        share = jnp.where(ids_wide[...] == e, ew_wide[...], 0.0)
        mix[e] = jnp.broadcast_to(jnp.sum(share, axis=1, keepdims=True), (SUB, LANES))

    peers(lambda other: q_copy(me, other).wait_recv())
    gathered = q_recv[...].astype(F32).reshape(shards, team, SUB, LANES)
    for one in range(team):
        q_heads[one] = gathered[:, one].reshape(shards * SUB, LANES).astype(BF16)
    loads[0].wait()
    loads[1].wait()
    for step in range(1, KV_HEADS):
        other, _ = column(step)
        for copy in key_copies(head, me, other):
            copy.wait_recv()

    n_cache = KV_HEADS * cache
    n_new = KV_HEADS * SUB
    fresh = new_recv[...].astype(F32)
    new_k = fresh[:, 0:SUB].reshape(n_new, LANES).astype(BF16)
    new_v = fresh[:, SUB : 2 * SUB].reshape(n_new, LANES).astype(BF16)
    lengths = fresh[:, rows_dev : rows_dev + 1, :]
    spot = lax.broadcasted_iota(jnp.int32, (KV_HEADS, cache, LANES), 1).astype(F32)
    cache_ok = (spot < lengths).reshape(n_cache, LANES)
    lane = lax.broadcasted_iota(jnp.int32, (n_new, LANES), 1)
    place = lax.broadcasted_iota(jnp.int32, (n_new, LANES), 0)
    row_of = (lane // SUB) * rows_dev + (lane % SUB) % rows_dev
    key_at = place % SUB
    span = ((place // SUB) * team + mate) * rows_dev + key_at
    new_ok = (key_at < rows_dev) & (span <= row_of)
    across = (((1,), (1,)), ((), ()))
    down = (((0,), (0,)), ((), ()))
    scale = HEAD_DIM ** (-0.5)
    stat_row = lax.broadcasted_iota(jnp.int32, (SUB, LANES), 0)

    def team_copies(target_mate, source_mate):
        target, source = head * team + target_mate, head * team + source_mate
        return (
            remote(NUM, num_send.at[target_mate], num_recv.at[source_mate], target, source),
            remote(STAT, stat_send.at[target_mate], stat_recv.at[source_mate], target, source),
        )

    def attend(step, carry):
        to = lax.rem(mate + step, team)
        queries = q_heads[to]
        keys = k_all[...].reshape(n_cache, LANES)
        old = lax.dot_general(keys, queries, across, preferred_element_type=F32) * scale
        new = lax.dot_general(new_k, queries, across, preferred_element_type=F32) * scale
        old = jnp.where(cache_ok, old, MASKED)
        new = jnp.where(new_ok, new, MASKED)
        top = jnp.maximum(
            jnp.max(old, axis=0, keepdims=True), jnp.max(new, axis=0, keepdims=True)
        )
        old = jnp.where(cache_ok, jnp.exp(old - top), 0.0)
        new = jnp.where(new_ok, jnp.exp(new - top), 0.0)
        total = jnp.sum(old, axis=0, keepdims=True) + jnp.sum(new, axis=0, keepdims=True)
        values = v_all[...].reshape(n_cache, LANES)
        numer = lax.dot_general(values, old.astype(BF16), down, preferred_element_type=F32)
        numer += lax.dot_general(new_v, new.astype(BF16), down, preferred_element_type=F32)
        num_send[to] = numer.astype(BF16)
        stat_send[to] = jnp.where(stat_row == 0, top, total)

        @pl.when(step < team)
        def _():
            for copy in team_copies(to, mate):
                copy.start()

        return carry

    lax.fori_loop(1, team + 1, attend, 0)
    num_recv[mate] = num_send[mate]
    stat_recv[mate] = stat_send[mate]
    for step in range(1, team):
        for copy in team_copies(mate, lax.rem(mate + step, team)):
            copy.wait_recv()
    tops = stat_recv[:, 0:1, :]
    weight = jnp.exp(tops - jnp.max(tops, axis=0, keepdims=True))
    weight = weight / jnp.sum(weight * stat_recv[:, 1:2, :], axis=0, keepdims=True)
    attention = jnp.sum(num_recv[...].astype(F32) * weight, axis=0).astype(BF16)

    n_tile = shards * SUB
    tile_row = lax.broadcasted_iota(jnp.int32, (n_tile, LANES), 0)
    tile_lane = lax.broadcasted_iota(jnp.int32, (n_tile, LANES), 1)
    odd = (tile_row % SUB) >= HALF
    own_row = tile_row % HALF
    parts = []
    for which in range(pair):
        pick = (
            (tile_row // SUB == tile_lane // SUB)
            & (own_row < rows_dev)
            & (tile_lane % SUB == which * rows_dev + own_row)
        )
        pick = jnp.where(pick, 1.0, 0.0).astype(BF16)
        parts.append(
            lax.dot_general(pick, attention, across, preferred_element_type=F32).astype(BF16)
        )
    columns = jnp.concatenate(parts, axis=1)

    def to_blocks(ref, at, tile):
        pieces = []
        for j in range(2):
            left = tile[:, 2 * j * LANES : (2 * j + 1) * LANES]
            right = tile[:, (2 * j + 1) * LANES : (2 * j + 2) * LANES]
            pieces.append(jnp.where(odd, right, left).reshape(shards, SUB, LANES))
        ref[:, at * 2 * SUB : (at + 1) * 2 * SUB, :] = jnp.concatenate(pieces, axis=1).astype(BF16)

    loads[2].wait()
    wide = 4 * LANES
    for at in range(width // wide):
        tile = jnp.dot(columns, wo[:, at * wide : (at + 1) * wide], preferred_element_type=F32)
        to_blocks(proj_send, at, tile)

    def proj_copy(target, source):
        return remote(PROJ, proj_send.at[target], proj_recv.at[source], target, source)

    peers(lambda other: proj_copy(other, me).start())
    proj_recv[me] = proj_send[me]
    peers(lambda other: proj_copy(me, other).wait_recv())
    state = res_wide[...] + jnp.sum(proj_recv[...].astype(F32), axis=0)
    state = state.reshape(chunks // 2, SUB, LANES)
    squares = jnp.sum(jnp.sum(state * state, axis=0), axis=1, keepdims=True)
    squares = squares + jnp.concatenate([squares[HALF:], squares[:HALF]], axis=0)
    normed = state * lax.rsqrt(squares / width + epsilon)[None]
    normed = normed.reshape(chunks * HALF, LANES) * gain_wide[...]
    row_send[...] = normed.astype(BF16)

    def row_copy(target, source):
        return remote(ROWS, row_send, row_recv.at[source], target, source)

    peers(lambda other: row_copy(other, me).start())
    row_recv[me] = row_send[...]
    peers(lambda other: row_copy(me, other).wait_recv())

    for at in range(chunks // 4):
        both = row_recv[:, at * 2 * SUB : (at + 1) * 2 * SUB, :].astype(F32)
        for j in range(2):
            piece = both[:, j * SUB : (j + 1) * SUB].reshape(n_tile, LANES)
            start = (4 * at + 2 * j) * LANES
            x_all[:, start : start + LANES] = jnp.where(odd, 0.0, piece).astype(BF16)
            x_all[:, start + LANES : start + 2 * LANES] = jnp.where(odd, piece, 0.0).astype(BF16)

    def fold(part):
        part = part.reshape(shards, SUB, part.shape[1])
        turned = jnp.concatenate([part[:, HALF:], part[:, :HALF]], axis=1)
        return (part + turned).reshape(n_tile, part.shape[2])

    loads[3].wait()
    loads[4].wait()
    hidden = act.shape[1]
    step_cols = 2 * LANES if hidden % (2 * LANES) == 0 else LANES
    for at in range(hidden // step_cols):
        lanes = slice(at * step_cols, (at + 1) * step_cols)
        gate = fold(jnp.dot(x_all[...], wg[:, lanes], preferred_element_type=F32))
        up = fold(jnp.dot(x_all[...], wu[:, lanes], preferred_element_type=F32))
        act[:, lanes] = (gate / (1.0 + jnp.exp(-gate)) * up).astype(BF16)
    loads[5].wait()
    for at in range(width // wide):
        tile = jnp.dot(act[...], wd[:, at * wide : (at + 1) * wide], preferred_element_type=F32)
        to_blocks(back_send, at, tile)

    def back_copy(target, source):
        return remote(BACK, back_send.at[target], back_recv.at[source], target, source)

    peers(lambda other: back_copy(other, me).start())
    back_recv[me] = back_send[me]

    for step in range(1, KV_HEADS):
        other, target = column(step)
        for copy in key_copies(other, target, head):
            copy.wait_send()
    for step in range(1, team):
        for copy in team_copies(lax.rem(mate + step, team), mate):
            copy.wait_send()

    def sent(other):
        q_copy(other, me).wait_send()
        proj_copy(other, me).wait_send()
        row_copy(other, me).wait_send()

    peers(sent)
    peers(lambda other: back_copy(me, other).wait_recv())

    def combine(e, total):
        block = back_recv[e].astype(F32).reshape(chunks // 2, SUB, LANES)
        return total + mix[e][None] * block

    final = lax.fori_loop(0, shards, combine, state).reshape(chunks * HALF, LANES)
    for c in range(chunks):
        out_ref[:, c * LANES : (c + 1) * LANES] = final[c * HALF : c * HALF + rows_dev].astype(BF16)
    peers(lambda other: back_copy(other, me).wait_send())


def local(*args):
    (queries, cache_keys, _, _, _, _, residual_in, out_weight, gain, expert_gate) = args[:10]
    shards = lax.axis_size("ctx")
    rows_dev, width = residual_in.shape
    capacity = max(2, 2 * rows_dev * TOP // shards)
    if not fits(shards, rows_dev, width, capacity, expert_gate.shape[0]):
        return plain(*args)
    team = shards // KV_HEADS
    hidden = expert_gate.shape[2]
    cache = cache_keys.shape[0]
    rows = width // LANES * HALF
    any_spec = pl.BlockSpec(memory_space=pl.ANY)
    vmem = pl.BlockSpec(memory_space=pltpu.VMEM)
    smem = pl.BlockSpec(memory_space=pltpu.SMEM)
    blocks = pltpu.VMEM((shards, rows, LANES), BF16)
    tiles = pltpu.VMEM((team, LANES, shards * SUB), BF16)
    stats = pltpu.VMEM((team, SUB, LANES), F32)
    keys = pltpu.VMEM((KV_HEADS, cache, LANES), BF16)
    new = pltpu.VMEM((KV_HEADS, 2 * SUB, LANES), BF16)
    flops = 2 * shards * SUB * width * (3 * hidden + out_weight.shape[0])
    return pl.pallas_call(
        functools.partial(layer_kernel, shards),
        out_shape=jax.ShapeDtypeStruct((rows_dev, width), BF16),
        in_specs=[
            vmem, any_spec, any_spec, vmem, vmem, smem, vmem,
            any_spec, vmem, any_spec, any_spec, any_spec, vmem, vmem,
        ],
        out_specs=vmem,
        scratch_shapes=[
            pltpu.VMEM(out_weight.shape, BF16),
            pltpu.VMEM((width, hidden), BF16),
            pltpu.VMEM((width, hidden), BF16),
            pltpu.VMEM((hidden, width), BF16),
            pltpu.VMEM((KV_HEADS, team * SUB, LANES), F32),
            pltpu.VMEM((KV_HEADS, team * SUB, LANES), BF16),
            pltpu.VMEM((shards, team * SUB, LANES), BF16),
            pltpu.VMEM((team, shards * SUB, LANES), BF16),
            keys,
            keys,
            pltpu.VMEM((KV_HEADS, 2 * SUB, LANES), F32),
            new,
            new,
            tiles,
            tiles,
            stats,
            stats,
            blocks,
            blocks,
            pltpu.VMEM((rows, LANES), F32),
            pltpu.VMEM((rows, LANES), F32),
            pltpu.VMEM((SUB, TOP), jnp.int32),
            pltpu.VMEM((SUB, TOP), F32),
            pltpu.VMEM((shards, SUB, LANES), F32),
            pltpu.VMEM((rows, LANES), BF16),
            blocks,
            pltpu.VMEM((shards * SUB, width), BF16),
            pltpu.VMEM((shards * SUB, hidden), BF16),
            blocks,
            blocks,
            pltpu.SemaphoreType.DMA((6,)),
            pltpu.SemaphoreType.DMA((9, shards)),
            pltpu.SemaphoreType.DMA((9, shards)),
        ],
        compiler_params=pltpu.CompilerParams(
            collective_id=0, has_side_effects=True, vmem_limit_bytes=40 * 1024 * 1024
        ),
        cost_estimate=pl.CostEstimate(
            flops=flops, bytes_accessed=2 * 3 * hidden * width, transcendentals=0
        ),
    )(*args[:8], gain.reshape(1, -1), *args[9:])


def solution(mesh):
    placed = (
        P(("groups", "ctx"), None),
        P(("groups", "ctx"), None),
        P(("groups", "ctx"), None),
        P(("groups", "ctx"), None),
        P(("groups", "ctx"), None),
        P(("groups", "ctx")),
        P(("groups", "ctx"), None),
        P("ctx", None),
        P(),
        P("ctx", None, None),
        P("ctx", None, None),
        P("ctx", None, None),
        P(("groups", "ctx"), None),
        P(("groups", "ctx"), None),
    )
    return jax.shard_map(
        local, mesh=mesh, in_specs=placed, out_specs=P(("groups", "ctx"), None), check_vma=False
    )
```

```python
import functools

import jax
import jax.numpy as jnp
from jax import lax
from jax.experimental import pallas as pl
from jax.experimental.pallas import tpu as pltpu
from jax.sharding import PartitionSpec as P

HEADS = 32
KV_HEADS = 4
HEAD_DIM = 128
TOP = 8


MASKED = -1e30
epsilon = 1e-06


def plain(
    queries,
    cache_keys,
    cache_values,
    new_keys,
    new_values,
    cache_lengths,
    residual_in,
    out_weight,
    norm_gain,
    expert_gate,
    expert_up,
    expert_down,
    expert_ids,
    expert_weights,
):
    shards = lax.axis_size("ctx")
    device = lax.axis_index("ctx")
    rows_dev = residual_in.shape[0]
    capacity = max(2, 2 * rows_dev * TOP // shards)
    group_size = HEADS // KV_HEADS
    whole_queries = lax.all_gather(queries, "ctx", axis=0, tiled=True)
    all_rows = whole_queries.shape[0]
    query_heads = whole_queries.reshape(all_rows, KV_HEADS, group_size, HEAD_DIM)
    local_cache = cache_keys.shape[0]
    key_rows = jnp.concatenate([cache_keys, new_keys], 0).reshape(
        local_cache + rows_dev, KV_HEADS, HEAD_DIM
    )
    value_rows = jnp.concatenate([cache_values, new_values], 0).reshape(
        local_cache + rows_dev, KV_HEADS, HEAD_DIM
    )
    slot_ids = jnp.arange(local_cache + rows_dev, dtype=jnp.int32)
    span_pos = device * rows_dev + slot_ids - local_cache
    row_ids = jnp.arange(all_rows, dtype=jnp.int32)
    usable = jnp.where(
        slot_ids[None, :] < local_cache,
        (slot_ids < cache_lengths[0])[None, :],
        span_pos[None, :] <= row_ids[:, None],
    )
    scores = jnp.einsum(
        "rkgd,nkd->kgrn", query_heads, key_rows, preferred_element_type=jnp.float32
    ) * HEAD_DIM ** (-0.5)
    scores = jnp.where(usable, scores, MASKED)
    maxima = jnp.max(scores, axis=-1)
    exp_weights = jnp.where(usable, jnp.exp(scores - maxima[..., None]), 0.0)
    totals = jnp.sum(exp_weights, axis=-1)
    numerators = jnp.einsum(
        "kgrn,nkd->rkgd",
        exp_weights.astype(jnp.bfloat16),
        value_rows,
        preferred_element_type=jnp.float32,
    ).reshape(all_rows, HEADS, HEAD_DIM)
    maxima = maxima.transpose(2, 0, 1).reshape(all_rows, HEADS)
    totals = totals.transpose(2, 0, 1).reshape(all_rows, HEADS)
    largest = lax.pmax(maxima, "ctx")
    rescale = jnp.exp(maxima - largest)
    denoms = lax.psum(totals * rescale, "ctx")
    weighted = (numerators * (rescale / denoms)[..., None]).reshape(all_rows, HEADS * HEAD_DIM)
    columns = lax.psum_scatter(weighted, "ctx", scatter_dimension=1, tiled=True).astype(
        jnp.bfloat16
    )
    projected = lax.psum_scatter(
        jnp.dot(columns, out_weight, preferred_element_type=jnp.float32),
        "ctx",
        scatter_dimension=0,
        tiled=True,
    )
    state = residual_in.astype(jnp.float32) + projected
    normed = (
        state
        * lax.rsqrt(jnp.mean(state * state, axis=1, keepdims=True) + epsilon)
        * norm_gain.astype(jnp.float32)
    ).astype(jnp.bfloat16)
    n_slots = shards * capacity
    flat_ids = expert_ids.reshape(-1)
    places = jnp.arange(flat_ids.shape[0], dtype=jnp.int32)
    earlier = (flat_ids[:, None] == flat_ids[None, :]) & (places[None, :] < places[:, None])
    slot_of = flat_ids * capacity + jnp.sum(earlier.astype(jnp.int32), axis=1)
    one_hot = (slot_of[:, None] == jnp.arange(n_slots, dtype=jnp.int32)[None, :]).astype(
        jnp.float32
    )
    dispatch_map = one_hot.reshape(rows_dev, TOP, n_slots).sum(1)
    outgoing = (
        jnp.dot(dispatch_map.T.astype(jnp.bfloat16), normed, preferred_element_type=jnp.float32)
        .astype(jnp.bfloat16)
        .reshape(shards, capacity, normed.shape[1])
    )
    received = lax.all_to_all(outgoing, "ctx", split_axis=0, concat_axis=0, tiled=True)
    gate_out = jnp.einsum(
        "scd,df->scf", received, expert_gate[0], preferred_element_type=jnp.float32
    )
    up_out = jnp.einsum("scd,df->scf", received, expert_up[0], preferred_element_type=jnp.float32)
    activated = (jax.nn.silu(gate_out) * up_out).astype(jnp.bfloat16)
    expert_out = jnp.einsum(
        "scf,fd->scd", activated, expert_down[0], preferred_element_type=jnp.float32
    ).astype(jnp.bfloat16)
    back = lax.all_to_all(expert_out, "ctx", split_axis=0, concat_axis=0, tiled=True)
    combine_map = (
        (one_hot * expert_weights.reshape(-1)[:, None]).reshape(rows_dev, TOP, n_slots).sum(1)
    )
    expert_sum = jnp.dot(
        combine_map,
        back.reshape(n_slots, normed.shape[1]).astype(jnp.float32),
        precision=lax.Precision.HIGHEST,
    )
    return (state + expert_sum).astype(jnp.bfloat16)


LANES = 128
SUB = 8
MESH = pl.DeviceIdType.MESH
F32 = jnp.float32
BF16 = jnp.bfloat16
Q, K, V, NEW, NUM, STAT, PROJ, ROWS, BACK = range(9)


def fits(shards, rows_dev, width, capacity, experts_dev):
    team = shards // KV_HEADS
    if shards % KV_HEADS or team == 0 or (HEADS // KV_HEADS) % team:
        return False
    pair = HEADS // KV_HEADS // team
    return (
        experts_dev == 1
        and team == KV_HEADS
        and HEAD_DIM == LANES
        and shards * SUB == LANES
        and (shards * rows_dev) % (2 * SUB) == 0
        and pair * rows_dev <= SUB
        and capacity >= rows_dev
        and width % (2 * SUB * LANES) == 0
    )


def layer_kernel(
    shards,
    q_hbm,
    ck_ref,
    cv_ref,
    nk_hbm,
    nv_hbm,
    len_ref,
    res_hbm,
    wo_ref,
    gain_hbm,
    wg_ref,
    wu_ref,
    wd_ref,
    ids_hbm,
    ew_hbm,
    out_ref,
    wo,
    wg,
    wu,
    wd,
    q_wide,
    q_send,
    q_recv,
    q_heads,
    k_all,
    v_all,
    new_wide,
    new_send,
    new_recv,
    num_send,
    num_recv,
    stat_send,
    stat_recv,
    stage,
    proj_send,
    proj_recv,
    res_wide,
    gain_wide,
    mix,
    row_send,
    row_recv,
    x_all,
    act,
    back_send,
    back_recv,
    q_ref,
    nk_ref,
    nv_ref,
    res_ref,
    gain_ref,
    ids_ref,
    ew_ref,
    load_sem,
    send_sem,
    recv_sem,
):
    me = lax.axis_index("ctx")
    team = shards // KV_HEADS
    pair = HEADS // KV_HEADS // team
    rows_dev, width = res_hbm.shape
    chunks = width // LANES
    cache = ck_ref.shape[0]
    plane, mate = me // team, me % team

    barrier = pltpu.get_barrier_semaphore()

    def greet(step, carry):
        pl.semaphore_signal(
            barrier, inc=1, device_id={"ctx": lax.rem(me + step, shards)}, device_id_type=MESH
        )
        return carry

    lax.fori_loop(1, shards, greet, 0)

    own_lanes = pl.ds(pl.multiple_of(mate * LANES, LANES), LANES)
    small = [
        (q_hbm, q_ref),
        (nk_hbm, nk_ref),
        (nv_hbm, nv_ref),
        (res_hbm, res_ref),
        (gain_hbm, gain_ref),
        (ids_hbm, ids_ref),
        (ew_hbm, ew_ref),
    ]
    large = [
        (ck_ref.at[:, own_lanes], k_all.at[mate]),
        (cv_ref.at[:, own_lanes], v_all.at[mate]),
        (wo_ref, wo),
        (wg_ref.at[0], wg),
        (wu_ref.at[0], wu),
        (wd_ref.at[0], wd),
    ]
    loads = [
        pltpu.make_async_copy(src, dst, load_sem.at[i])
        for i, (src, dst) in enumerate(small + large)
    ]
    for load in loads:
        load.start()
    for load in loads[: len(small)]:
        load.wait()
    loads = loads[len(small) :]

    q_wide[...] = jnp.zeros_like(q_wide)
    for one in range(HEADS):
        kv, rest = divmod(one, HEADS // KV_HEADS)
        who, which = divmod(rest, pair)
        q_wide[kv, pl.ds(who * SUB + which * rows_dev, rows_dev), :] = q_ref[
            :, one * LANES : (one + 1) * LANES
        ].astype(F32)
    q_send[...] = q_wide[...].astype(BF16)
    new_wide[...] = jnp.zeros_like(new_wide)
    live = jnp.full((1, LANES), len_ref[0], jnp.int32).astype(F32)
    for kv in range(KV_HEADS):
        lanes = slice(kv * LANES, (kv + 1) * LANES)
        new_wide[kv, 0:rows_dev, :] = nk_ref[:, lanes].astype(F32)
        new_wide[kv, rows_dev : rows_dev + 1, :] = live
        new_wide[kv, SUB : SUB + rows_dev, :] = nv_ref[:, lanes].astype(F32)
    new_send[...] = new_wide[...].astype(BF16)

    def remote(kind, src, dst, target, source):
        return pltpu.make_async_remote_copy(
            src_ref=src,
            dst_ref=dst,
            send_sem=send_sem.at[kind, target],
            recv_sem=recv_sem.at[kind, source],
            device_id={"ctx": target},
            device_id_type=MESH,
        )

    def near(step):
        other = lax.rem(mate + step, team)
        return other, plane * team + other

    def key_copies(lane_head, target, source_mate):
        lanes = pl.ds(pl.multiple_of(lane_head * LANES, LANES), LANES)
        source = plane * team + source_mate
        return (
            remote(K, ck_ref.at[:, lanes], k_all.at[source_mate], target, source),
            remote(V, cv_ref.at[:, lanes], v_all.at[source_mate], target, source),
            remote(NEW, new_send.at[lane_head], new_recv.at[source_mate], target, source),
        )

    pl.semaphore_wait(barrier, shards - 1)

    def peers(body):
        def step_body(step, carry):
            body(lax.rem(me + step, shards))
            return carry

        lax.fori_loop(1, shards, step_body, 0)

    def q_copy(target, source):
        return remote(Q, q_send.at[target % team], q_recv.at[source], target, source)

    peers(lambda other: q_copy(other, me).start())
    for step in range(1, team):
        for copy in key_copies(*near(step), mate):
            copy.start()

    q_recv[me] = q_send[mate]
    new_recv[mate] = new_send[mate]

    for c in range(chunks):
        lanes = slice(c * LANES, (c + 1) * LANES)
        res_wide[pl.ds(c, rows_dev, stride=chunks), :] = res_ref[:, lanes].astype(F32)
        gain_wide[c : c + 1, :] = gain_ref[lanes].astype(F32).reshape(1, LANES)
    for e in range(shards):
        share = jnp.where(ids_ref[...] == e, ew_ref[...], 0.0)
        mix[e, 0:rows_dev, :] = jnp.broadcast_to(
            jnp.sum(share, axis=1, keepdims=True), (rows_dev, LANES)
        )

    peers(lambda other: q_copy(me, other).wait_recv())
    gathered = q_recv[...].astype(F32).reshape(shards, team, SUB, LANES)
    for one in range(team):
        q_heads[one] = gathered[:, one].reshape(shards * SUB, LANES).astype(BF16)
    loads[0].wait()
    loads[1].wait()
    for step in range(1, team):
        other, _ = near(step)
        for copy in key_copies(mate, me, other):
            copy.wait_recv()

    n_cache = team * cache
    n_new = team * SUB
    fresh = new_recv[...].astype(F32)
    new_k = fresh[:, 0:SUB].reshape(n_new, LANES).astype(BF16)
    new_v = fresh[:, SUB : 2 * SUB].reshape(n_new, LANES).astype(BF16)
    lengths = fresh[:, rows_dev : rows_dev + 1, :]
    spot = lax.broadcasted_iota(jnp.int32, (team, cache, LANES), 1).astype(F32)
    cache_ok = (spot < lengths).reshape(n_cache, LANES)
    lane = lax.broadcasted_iota(jnp.int32, (n_new, LANES), 1)
    place = lax.broadcasted_iota(jnp.int32, (n_new, LANES), 0)
    row_of = (lane // SUB) * rows_dev + (lane % SUB) % rows_dev
    key_at = place % SUB
    span = (plane * team + place // SUB) * rows_dev + key_at
    new_ok = (key_at < rows_dev) & (span <= row_of)
    across = (((1,), (1,)), ((), ()))
    down = (((0,), (0,)), ((), ()))
    scale = HEAD_DIM ** (-0.5)
    stat_row = lax.broadcasted_iota(jnp.int32, (SUB, LANES), 0)

    def head_copies(target, target_mate, source, source_plane):
        return (
            remote(NUM, num_send.at[target_mate], num_recv.at[source_plane], target, source),
            remote(STAT, stat_send.at[target_mate], stat_recv.at[source_plane], target, source),
        )

    def attend(step, carry):
        to = lax.rem(plane + step, team)
        queries = q_heads[to]
        keys = k_all[...].reshape(n_cache, LANES)
        old = lax.dot_general(keys, queries, across, preferred_element_type=F32) * scale
        new = lax.dot_general(new_k, queries, across, preferred_element_type=F32) * scale
        old = jnp.where(cache_ok, old, MASKED)
        new = jnp.where(new_ok, new, MASKED)
        top = jnp.maximum(
            jnp.max(old, axis=0, keepdims=True), jnp.max(new, axis=0, keepdims=True)
        )
        old = jnp.where(cache_ok, jnp.exp(old - top), 0.0)
        new = jnp.where(new_ok, jnp.exp(new - top), 0.0)
        total = jnp.sum(old, axis=0, keepdims=True) + jnp.sum(new, axis=0, keepdims=True)
        values = v_all[...].reshape(n_cache, LANES)
        numer = lax.dot_general(values, old.astype(BF16), down, preferred_element_type=F32)
        numer += lax.dot_general(new_v, new.astype(BF16), down, preferred_element_type=F32)
        num_send[to] = numer.astype(BF16)
        stat_send[to] = jnp.where(stat_row == 0, top, total)

        target = mate * team + to

        @pl.when(target != me)
        def _():
            for copy in head_copies(target, to, me, plane):
                copy.start()

        @pl.when(target == me)
        def _():
            num_recv[plane] = num_send[to]
            stat_recv[plane] = stat_send[to]

        return carry

    lax.fori_loop(0, team, attend, 0)
    for at in range(team):
        source = at * team + plane

        @pl.when(source != me)
        def _():
            for copy in head_copies(me, mate, source, at):
                copy.wait_recv()

    tops = stat_recv[:, 0:1, :]
    weight = jnp.exp(tops - jnp.max(tops, axis=0, keepdims=True))
    weight = weight / jnp.sum(weight * stat_recv[:, 1:2, :], axis=0, keepdims=True)
    attention = jnp.sum(num_recv[...].astype(F32) * weight, axis=0).astype(BF16)

    n_rows = shards * rows_dev
    tile_row = lax.broadcasted_iota(jnp.int32, (n_rows, LANES), 0)
    tile_lane = lax.broadcasted_iota(jnp.int32, (n_rows, LANES), 1)
    parts = []
    for which in range(pair):
        pick = (tile_row // rows_dev == tile_lane // SUB) & (
            tile_lane % SUB == which * rows_dev + tile_row % rows_dev
        )
        pick = jnp.where(pick, 1.0, 0.0).astype(BF16)
        parts.append(
            lax.dot_general(pick, attention, across, preferred_element_type=F32).astype(BF16)
        )
    columns = jnp.concatenate(parts, axis=1)

    def spread(first, tile):
        for j in range(tile.shape[1] // LANES):
            stage[pl.ds(first + j, n_rows, stride=chunks), :] = tile[
                :, j * LANES : (j + 1) * LANES
            ]

    loads[2].wait()
    wide = 4 * LANES
    for at in range(width // wide):
        tile = jnp.dot(columns, wo[:, at * wide : (at + 1) * wide], preferred_element_type=F32)
        spread(4 * at, tile)
    proj_send[...] = stage[...].reshape(proj_send.shape).astype(BF16)

    def proj_copy(target, source):
        return remote(PROJ, proj_send.at[target], proj_recv.at[source], target, source)

    peers(lambda other: proj_copy(other, me).start())
    proj_recv[me] = proj_send[me]
    peers(lambda other: proj_copy(me, other).wait_recv())
    state = res_wide[...] + jnp.sum(proj_recv[...].astype(F32), axis=0)
    state = state.reshape(rows_dev, chunks, LANES)
    squares = jnp.sum(jnp.sum(state * state, axis=1, keepdims=True), axis=2, keepdims=True)
    normed = state * lax.rsqrt(squares / width + epsilon) * gain_wide[...][None]
    normed = normed.reshape(rows_dev * chunks, LANES)
    row_send[...] = normed.astype(BF16)

    def row_copy(target, source):
        return remote(ROWS, row_send, row_recv.at[source], target, source)

    peers(lambda other: row_copy(other, me).start())
    row_recv[me] = row_send[...]
    peers(lambda other: row_copy(me, other).wait_recv())

    stage[...] = row_recv[...].astype(F32).reshape(stage.shape)
    for c in range(chunks):
        x_all[:, c * LANES : (c + 1) * LANES] = stage[
            pl.ds(c, n_rows, stride=chunks), :
        ].astype(BF16)

    loads[3].wait()
    loads[4].wait()
    hidden = act.shape[1]
    step_cols = 2 * LANES if hidden % (2 * LANES) == 0 else LANES
    for at in range(hidden // step_cols):
        lanes = slice(at * step_cols, (at + 1) * step_cols)
        gate = jnp.dot(x_all[...], wg[:, lanes], preferred_element_type=F32)
        up = jnp.dot(x_all[...], wu[:, lanes], preferred_element_type=F32)
        act[:, lanes] = (gate / (1.0 + jnp.exp(-gate)) * up).astype(BF16)
    loads[5].wait()
    for at in range(width // wide):
        tile = jnp.dot(act[...], wd[:, at * wide : (at + 1) * wide], preferred_element_type=F32)
        spread(4 * at, tile)
    back_send[...] = stage[...].reshape(back_send.shape).astype(BF16)

    def back_copy(target, source):
        return remote(BACK, back_send.at[target], back_recv.at[source], target, source)

    peers(lambda other: back_copy(other, me).start())
    back_recv[me] = back_send[me]

    for step in range(1, team):
        for copy in key_copies(*near(step), mate):
            copy.wait_send()
    for at in range(team):
        target = mate * team + at

        @pl.when(target != me)
        def _():
            for copy in head_copies(target, at, me, plane):
                copy.wait_send()

    def sent(other):
        q_copy(other, me).wait_send()
        proj_copy(other, me).wait_send()
        row_copy(other, me).wait_send()

    peers(sent)
    peers(lambda other: back_copy(me, other).wait_recv())

    def combine(e, total):
        block = back_recv[e].astype(F32).reshape(rows_dev, chunks, LANES)
        share = mix[e]
        return tuple(total[r] + share[r : r + 1, :] * block[r] for r in range(rows_dev))

    final = lax.fori_loop(0, shards, combine, tuple(state[r] for r in range(rows_dev)))
    for r in range(rows_dev):
        res_wide[r * chunks : (r + 1) * chunks, :] = final[r]
    for c in range(chunks):
        out_ref[:, c * LANES : (c + 1) * LANES] = res_wide[
            pl.ds(c, rows_dev, stride=chunks), :
        ].astype(BF16)
    peers(lambda other: back_copy(other, me).wait_send())


def local(*args):
    (queries, cache_keys, _, _, _, _, residual_in, out_weight, _, expert_gate) = args[:10]
    shards = lax.axis_size("ctx")
    rows_dev, width = residual_in.shape
    capacity = max(2, 2 * rows_dev * TOP // shards)
    if not fits(shards, rows_dev, width, capacity, expert_gate.shape[0]):
        return plain(*args)
    team = shards // KV_HEADS
    hidden = expert_gate.shape[2]
    cache = cache_keys.shape[0]
    rows = rows_dev * width // LANES
    any_spec = pl.BlockSpec(memory_space=pl.ANY)
    vmem = pl.BlockSpec(memory_space=pltpu.VMEM)
    smem = pl.BlockSpec(memory_space=pltpu.SMEM)
    blocks = pltpu.VMEM((shards, rows, LANES), BF16)
    tiles = pltpu.VMEM((team, LANES, shards * SUB), BF16)
    stats = pltpu.VMEM((team, SUB, LANES), F32)
    keys = pltpu.VMEM((team, cache, LANES), BF16)
    new = pltpu.VMEM((KV_HEADS, 2 * SUB, LANES), BF16)
    flops = 2 * shards * rows_dev * width * (3 * hidden + out_weight.shape[0])
    return pl.pallas_call(
        functools.partial(layer_kernel, shards),
        out_shape=jax.ShapeDtypeStruct((rows_dev, width), BF16),
        in_specs=[any_spec] * 5 + [smem] + [any_spec] * 8,
        out_specs=vmem,
        scratch_shapes=[
            pltpu.VMEM(out_weight.shape, BF16),
            pltpu.VMEM((width, hidden), BF16),
            pltpu.VMEM((width, hidden), BF16),
            pltpu.VMEM((hidden, width), BF16),
            pltpu.VMEM((KV_HEADS, team * SUB, LANES), F32),
            pltpu.VMEM((KV_HEADS, team * SUB, LANES), BF16),
            pltpu.VMEM((shards, team * SUB, LANES), BF16),
            pltpu.VMEM((team, shards * SUB, LANES), BF16),
            keys,
            keys,
            pltpu.VMEM((KV_HEADS, 2 * SUB, LANES), F32),
            new,
            new,
            tiles,
            tiles,
            stats,
            stats,
            pltpu.VMEM((shards * rows, LANES), F32),
            blocks,
            blocks,
            pltpu.VMEM((rows, LANES), F32),
            pltpu.VMEM((width // LANES, LANES), F32),
            pltpu.VMEM((shards, SUB, LANES), F32),
            pltpu.VMEM((rows, LANES), BF16),
            blocks,
            pltpu.VMEM((shards * rows_dev, width), BF16),
            pltpu.VMEM((shards * rows_dev, hidden), BF16),
            blocks,
            blocks,
            *(pltpu.VMEM(args[i].shape, args[i].dtype) for i in (0, 3, 4, 6)),
            pltpu.VMEM((width,), BF16),
            *(pltpu.VMEM(args[i].shape, args[i].dtype) for i in (12, 13)),
            pltpu.SemaphoreType.DMA((13,)),
            pltpu.SemaphoreType.DMA((9, shards)),
            pltpu.SemaphoreType.DMA((9, shards)),
        ],
        compiler_params=pltpu.CompilerParams(
            collective_id=0, has_side_effects=True, vmem_limit_bytes=60 * 1024 * 1024
        ),
        cost_estimate=pl.CostEstimate(
            flops=flops, bytes_accessed=2 * 3 * hidden * width, transcendentals=0
        ),
    )(*args)


def solution(mesh):
    placed = (
        P(("groups", "ctx"), None),
        P(("groups", "ctx"), None),
        P(("groups", "ctx"), None),
        P(("groups", "ctx"), None),
        P(("groups", "ctx"), None),
        P(("groups", "ctx")),
        P(("groups", "ctx"), None),
        P("ctx", None),
        P(),
        P("ctx", None, None),
        P("ctx", None, None),
        P("ctx", None, None),
        P(("groups", "ctx"), None),
        P(("groups", "ctx"), None),
    )
    return jax.shard_map(
        local, mesh=mesh, in_specs=placed, out_specs=P(("groups", "ctx"), None), check_vma=False
    )
```

```python
import functools

import jax
import jax.numpy as jnp
from jax import lax
from jax.experimental import pallas as pl
from jax.experimental.pallas import tpu as pltpu
from jax.sharding import PartitionSpec as P

HEADS = 32
KV_HEADS = 4
HEAD_DIM = 128
TOP = 8


MASKED = -1e30
epsilon = 1e-06


def plain(
    queries,
    cache_keys,
    cache_values,
    new_keys,
    new_values,
    cache_lengths,
    residual_in,
    out_weight,
    norm_gain,
    expert_gate,
    expert_up,
    expert_down,
    expert_ids,
    expert_weights,
):
    shards = lax.axis_size("ctx")
    device = lax.axis_index("ctx")
    rows_dev = residual_in.shape[0]
    capacity = max(2, 2 * rows_dev * TOP // shards)
    group_size = HEADS // KV_HEADS
    whole_queries = lax.all_gather(queries, "ctx", axis=0, tiled=True)
    all_rows = whole_queries.shape[0]
    query_heads = whole_queries.reshape(all_rows, KV_HEADS, group_size, HEAD_DIM)
    local_cache = cache_keys.shape[0]
    key_rows = jnp.concatenate([cache_keys, new_keys], 0).reshape(
        local_cache + rows_dev, KV_HEADS, HEAD_DIM
    )
    value_rows = jnp.concatenate([cache_values, new_values], 0).reshape(
        local_cache + rows_dev, KV_HEADS, HEAD_DIM
    )
    slot_ids = jnp.arange(local_cache + rows_dev, dtype=jnp.int32)
    span_pos = device * rows_dev + slot_ids - local_cache
    row_ids = jnp.arange(all_rows, dtype=jnp.int32)
    usable = jnp.where(
        slot_ids[None, :] < local_cache,
        (slot_ids < cache_lengths[0])[None, :],
        span_pos[None, :] <= row_ids[:, None],
    )
    scores = jnp.einsum(
        "rkgd,nkd->kgrn", query_heads, key_rows, preferred_element_type=jnp.float32
    ) * HEAD_DIM ** (-0.5)
    scores = jnp.where(usable, scores, MASKED)
    maxima = jnp.max(scores, axis=-1)
    exp_weights = jnp.where(usable, jnp.exp(scores - maxima[..., None]), 0.0)
    totals = jnp.sum(exp_weights, axis=-1)
    numerators = jnp.einsum(
        "kgrn,nkd->rkgd",
        exp_weights.astype(jnp.bfloat16),
        value_rows,
        preferred_element_type=jnp.float32,
    ).reshape(all_rows, HEADS, HEAD_DIM)
    maxima = maxima.transpose(2, 0, 1).reshape(all_rows, HEADS)
    totals = totals.transpose(2, 0, 1).reshape(all_rows, HEADS)
    largest = lax.pmax(maxima, "ctx")
    rescale = jnp.exp(maxima - largest)
    denoms = lax.psum(totals * rescale, "ctx")
    weighted = (numerators * (rescale / denoms)[..., None]).reshape(all_rows, HEADS * HEAD_DIM)
    columns = lax.psum_scatter(weighted, "ctx", scatter_dimension=1, tiled=True).astype(
        jnp.bfloat16
    )
    projected = lax.psum_scatter(
        jnp.dot(columns, out_weight, preferred_element_type=jnp.float32),
        "ctx",
        scatter_dimension=0,
        tiled=True,
    )
    state = residual_in.astype(jnp.float32) + projected
    normed = (
        state
        * lax.rsqrt(jnp.mean(state * state, axis=1, keepdims=True) + epsilon)
        * norm_gain.astype(jnp.float32)
    ).astype(jnp.bfloat16)
    n_slots = shards * capacity
    flat_ids = expert_ids.reshape(-1)
    places = jnp.arange(flat_ids.shape[0], dtype=jnp.int32)
    earlier = (flat_ids[:, None] == flat_ids[None, :]) & (places[None, :] < places[:, None])
    slot_of = flat_ids * capacity + jnp.sum(earlier.astype(jnp.int32), axis=1)
    one_hot = (slot_of[:, None] == jnp.arange(n_slots, dtype=jnp.int32)[None, :]).astype(
        jnp.float32
    )
    dispatch_map = one_hot.reshape(rows_dev, TOP, n_slots).sum(1)
    outgoing = (
        jnp.dot(dispatch_map.T.astype(jnp.bfloat16), normed, preferred_element_type=jnp.float32)
        .astype(jnp.bfloat16)
        .reshape(shards, capacity, normed.shape[1])
    )
    received = lax.all_to_all(outgoing, "ctx", split_axis=0, concat_axis=0, tiled=True)
    gate_out = jnp.einsum(
        "scd,df->scf", received, expert_gate[0], preferred_element_type=jnp.float32
    )
    up_out = jnp.einsum("scd,df->scf", received, expert_up[0], preferred_element_type=jnp.float32)
    activated = (jax.nn.silu(gate_out) * up_out).astype(jnp.bfloat16)
    expert_out = jnp.einsum(
        "scf,fd->scd", activated, expert_down[0], preferred_element_type=jnp.float32
    ).astype(jnp.bfloat16)
    back = lax.all_to_all(expert_out, "ctx", split_axis=0, concat_axis=0, tiled=True)
    combine_map = (
        (one_hot * expert_weights.reshape(-1)[:, None]).reshape(rows_dev, TOP, n_slots).sum(1)
    )
    expert_sum = jnp.dot(
        combine_map,
        back.reshape(n_slots, normed.shape[1]).astype(jnp.float32),
        precision=lax.Precision.HIGHEST,
    )
    return (state + expert_sum).astype(jnp.bfloat16)


LANES = 128
SUB = 8
MESH = pl.DeviceIdType.MESH
F32 = jnp.float32
BF16 = jnp.bfloat16
Q, K, V, NEW, NUM, STAT, PROJ, ROWS, BACK, PROJ_PAIR, ROWS_PAIR, BACK_PAIR = range(12)
KINDS = 12


def fits(shards, rows_dev, width, capacity, experts_dev):
    team = shards // KV_HEADS
    if shards % KV_HEADS or team == 0 or (HEADS // KV_HEADS) % team:
        return False
    pair = HEADS // KV_HEADS // team
    return (
        experts_dev == 1
        and team == KV_HEADS
        and HEAD_DIM == LANES
        and shards * SUB == LANES
        and (shards * rows_dev) % (2 * SUB) == 0
        and pair * rows_dev <= SUB - 2
        and rows_dev <= team
        and shards <= LANES
        and capacity >= rows_dev
        and width % (2 * SUB * LANES) == 0
    )


def layer_kernel(
    shards,
    q_hbm,
    ck_ref,
    cv_ref,
    nk_hbm,
    nv_hbm,
    len_ref,
    res_hbm,
    wo_ref,
    gain_hbm,
    wg_ref,
    wu_ref,
    wd_ref,
    ids_hbm,
    ew_hbm,
    out_ref,
    wo,
    wg,
    wu,
    wd,
    q_wide,
    q_send,
    q_recv,
    q_heads,
    k_all,
    v_all,
    new_wide,
    new_send,
    new_recv,
    num_send,
    num_recv,
    stat_send,
    stat_recv,
    stage,
    proj_away,
    proj_near,
    proj_send,
    proj_recv,
    res_wide,
    gain_wide,
    mix_all,
    mix,
    row_send,
    row_recv,
    x_all,
    act,
    back_away,
    back_near,
    back_send,
    back_recv,
    q_ref,
    nk_ref,
    nv_ref,
    res_ref,
    gain_ref,
    ids_ref,
    ew_ref,
    load_sem,
    send_sem,
    recv_sem,
):
    me = lax.axis_index("ctx")
    team = shards // KV_HEADS
    pair = HEADS // KV_HEADS // team
    rows_dev, width = res_hbm.shape
    chunks = width // LANES
    cache = ck_ref.shape[0]
    plane, mate = me // team, me % team
    chips = shards // 2
    chip, core = me // 2, me % 2
    sibling = me + 1 - 2 * core

    barrier = pltpu.get_barrier_semaphore()

    def greet(step, carry):
        pl.semaphore_signal(
            barrier, inc=1, device_id={"ctx": lax.rem(me + step, shards)}, device_id_type=MESH
        )
        return carry

    lax.fori_loop(1, shards, greet, 0)

    own_lanes = pl.ds(pl.multiple_of(mate * LANES, LANES), LANES)
    small = [
        (q_hbm, q_ref),
        (nk_hbm, nk_ref),
        (nv_hbm, nv_ref),
        (res_hbm, res_ref),
        (gain_hbm, gain_ref),
        (ids_hbm, ids_ref),
        (ew_hbm, ew_ref),
    ]
    large = [
        (ck_ref.at[:, own_lanes], k_all.at[mate]),
        (cv_ref.at[:, own_lanes], v_all.at[mate]),
        (wo_ref, wo),
        (wg_ref.at[0], wg),
        (wu_ref.at[0], wu),
        (wd_ref.at[0], wd),
    ]
    loads = [
        pltpu.make_async_copy(src, dst, load_sem.at[i])
        for i, (src, dst) in enumerate(small + large)
    ]
    early = len(small) + 2
    for load in loads[:early]:
        load.start()
    for load in loads[: len(small)]:
        load.wait()

    q_wide[...] = jnp.zeros_like(q_wide)
    for one in range(HEADS):
        kv, rest = divmod(one, HEADS // KV_HEADS)
        who, which = divmod(rest, pair)
        q_wide[kv, pl.ds(who * SUB + which * rows_dev, rows_dev), :] = q_ref[
            :, one * LANES : (one + 1) * LANES
        ].astype(F32)
    expert = lax.broadcasted_iota(jnp.int32, (rows_dev, LANES), 1)
    routed = jnp.zeros((rows_dev, LANES), F32)
    for k in range(TOP):
        routed += jnp.where(expert == ids_ref[:, k : k + 1], ew_ref[:, k : k + 1], 0.0)
    coarse = routed.astype(BF16).astype(F32)
    fine = routed - coarse
    for kv in range(KV_HEADS):
        for r in range(rows_dev):
            q_wide[kv, (r + 1) * SUB - 2 : (r + 1) * SUB - 1, :] = coarse[r : r + 1]
            q_wide[kv, (r + 1) * SUB - 1 : (r + 1) * SUB, :] = fine[r : r + 1]
    q_send[...] = q_wide[...].astype(BF16)
    new_wide[...] = jnp.zeros_like(new_wide)
    live = jnp.full((1, LANES), len_ref[0], jnp.int32).astype(F32)
    for kv in range(KV_HEADS):
        lanes = slice(kv * LANES, (kv + 1) * LANES)
        new_wide[kv, 0:rows_dev, :] = nk_ref[:, lanes].astype(F32)
        new_wide[kv, rows_dev : rows_dev + 1, :] = live
        new_wide[kv, SUB : SUB + rows_dev, :] = nv_ref[:, lanes].astype(F32)
    new_send[...] = new_wide[...].astype(BF16)

    def remote(kind, src, dst, target, source):
        return pltpu.make_async_remote_copy(
            src_ref=src,
            dst_ref=dst,
            send_sem=send_sem.at[kind, target],
            recv_sem=recv_sem.at[kind, source],
            device_id={"ctx": target},
            device_id_type=MESH,
        )

    def near(step):
        other = lax.rem(mate + step, team)
        return other, plane * team + other

    def key_copies(lane_head, target, source_mate):
        lanes = pl.ds(pl.multiple_of(lane_head * LANES, LANES), LANES)
        source = plane * team + source_mate
        return (
            remote(K, ck_ref.at[:, lanes], k_all.at[source_mate], target, source),
            remote(V, cv_ref.at[:, lanes], v_all.at[source_mate], target, source),
            remote(NEW, new_send.at[lane_head], new_recv.at[source_mate], target, source),
        )

    pl.semaphore_wait(barrier, shards - 1)

    def peers(body):
        def step_body(step, carry):
            body(lax.rem(me + step, shards))
            return carry

        lax.fori_loop(1, shards, step_body, 0)

    def q_copy(target, source):
        return remote(Q, q_send.at[target % team], q_recv.at[source], target, source)

    peers(lambda other: q_copy(other, me).start())
    for step in range(1, team):
        for copy in key_copies(*near(step), mate):
            copy.start()
    for load in loads[early:]:
        load.start()
    loads = loads[len(small) :]

    q_recv[me] = q_send[mate]
    new_recv[mate] = new_send[mate]

    for c in range(chunks):
        lanes = slice(c * LANES, (c + 1) * LANES)
        res_wide[pl.ds(c, rows_dev, stride=chunks), :] = res_ref[:, lanes].astype(F32)
        gain_wide[c : c + 1, :] = gain_ref[lanes].astype(F32).reshape(1, LANES)

    peers(lambda other: q_copy(me, other).wait_recv())
    gathered = q_recv[...].astype(F32).reshape(shards, team, SUB, LANES)
    for one in range(team):
        q_heads[one] = gathered[:, one].reshape(shards * SUB, LANES).astype(BF16)
    at_lane = lax.broadcasted_iota(jnp.int32, (shards, LANES), 1)
    for r in range(rows_dev):
        both = gathered[:, r, SUB - 2, :] + gathered[:, r, SUB - 1, :]
        mine = jnp.sum(jnp.where(at_lane == me, both, 0.0), axis=1, keepdims=True)
        mix_all[...] = jnp.broadcast_to(mine, (shards, LANES))
        for half in range(2):
            mix[pl.ds(half * chips * rows_dev + r, chips, stride=rows_dev), :] = mix_all[
                pl.ds(half, chips, stride=2), :
            ]
    loads[0].wait()
    loads[1].wait()
    for step in range(1, team):
        other, _ = near(step)
        for copy in key_copies(mate, me, other):
            copy.wait_recv()

    n_cache = team * cache
    n_new = team * SUB
    fresh = new_recv[...].astype(F32)
    new_k = fresh[:, 0:SUB].reshape(n_new, LANES).astype(BF16)
    new_v = fresh[:, SUB : 2 * SUB].reshape(n_new, LANES).astype(BF16)
    lengths = fresh[:, rows_dev : rows_dev + 1, :]
    spot = lax.broadcasted_iota(jnp.int32, (team, cache, LANES), 1).astype(F32)
    cache_ok = (spot < lengths).reshape(n_cache, LANES)
    lane = lax.broadcasted_iota(jnp.int32, (n_new, LANES), 1)
    place = lax.broadcasted_iota(jnp.int32, (n_new, LANES), 0)
    row_of = (lane // SUB) * rows_dev + (lane % SUB) % rows_dev
    key_at = place % SUB
    span = (plane * team + place // SUB) * rows_dev + key_at
    new_ok = (key_at < rows_dev) & (span <= row_of)
    across = (((1,), (1,)), ((), ()))
    down = (((0,), (0,)), ((), ()))
    scale = HEAD_DIM ** (-0.5)
    stat_row = lax.broadcasted_iota(jnp.int32, (SUB, LANES), 0)

    def head_copies(target, target_mate, source, source_plane):
        return (
            remote(NUM, num_send.at[target_mate], num_recv.at[source_plane], target, source),
            remote(STAT, stat_send.at[target_mate], stat_recv.at[source_plane], target, source),
        )

    def attend(step, carry):
        to = lax.rem(plane + step, team)
        queries = q_heads[to]
        keys = k_all[...].reshape(n_cache, LANES)
        old = lax.dot_general(keys, queries, across, preferred_element_type=F32) * scale
        new = lax.dot_general(new_k, queries, across, preferred_element_type=F32) * scale
        old = jnp.where(cache_ok, old, MASKED)
        new = jnp.where(new_ok, new, MASKED)
        top = jnp.maximum(
            jnp.max(old, axis=0, keepdims=True), jnp.max(new, axis=0, keepdims=True)
        )
        old = jnp.where(cache_ok, jnp.exp(old - top), 0.0)
        new = jnp.where(new_ok, jnp.exp(new - top), 0.0)
        total = jnp.sum(old, axis=0, keepdims=True) + jnp.sum(new, axis=0, keepdims=True)
        values = v_all[...].reshape(n_cache, LANES)
        numer = lax.dot_general(values, old.astype(BF16), down, preferred_element_type=F32)
        numer += lax.dot_general(new_v, new.astype(BF16), down, preferred_element_type=F32)
        num_send[to] = numer.astype(BF16)
        stat_send[to] = jnp.where(stat_row == 0, top, total)

        target = mate * team + to

        @pl.when(target != me)
        def _():
            for copy in head_copies(target, to, me, plane):
                copy.start()

        @pl.when(target == me)
        def _():
            num_recv[plane] = num_send[to]
            stat_recv[plane] = stat_send[to]

        return carry

    lax.fori_loop(0, team, attend, 0)
    for at in range(team):
        source = at * team + plane

        @pl.when(source != me)
        def _():
            for copy in head_copies(me, mate, source, at):
                copy.wait_recv()

    tops = stat_recv[:, 0:1, :]
    weight = jnp.exp(tops - jnp.max(tops, axis=0, keepdims=True))
    weight = weight / jnp.sum(weight * stat_recv[:, 1:2, :], axis=0, keepdims=True)
    attention = jnp.sum(num_recv[...].astype(F32) * weight, axis=0).astype(BF16)

    n_rows = shards * rows_dev
    tile_row = lax.broadcasted_iota(jnp.int32, (n_rows, LANES), 0)
    tile_lane = lax.broadcasted_iota(jnp.int32, (n_rows, LANES), 1)
    tile_place = tile_row // rows_dev
    tile_device = (tile_place % chips) * 2 + tile_place // chips
    parts = []
    for which in range(pair):
        pick = (tile_device == tile_lane // SUB) & (
            tile_lane % SUB == which * rows_dev + tile_row % rows_dev
        )
        pick = jnp.where(pick, 1.0, 0.0).astype(BF16)
        parts.append(
            lax.dot_general(pick, attention, across, preferred_element_type=F32).astype(BF16)
        )
    columns = jnp.concatenate(parts, axis=1)

    def spread(first, tile):
        for j in range(tile.shape[1] // LANES):
            stage[pl.ds(first + j, n_rows, stride=chunks), :] = tile[
                :, j * LANES : (j + 1) * LANES
            ]

    loads[2].wait()
    wide = 4 * LANES
    for at in range(width // wide):
        tile = jnp.dot(columns, wo[:, at * wide : (at + 1) * wide], preferred_element_type=F32)
        spread(4 * at, tile)

    half_rows = chips * rows_dev * chunks
    own_half = pl.ds(pl.multiple_of(core * half_rows, half_rows), half_rows)
    away_half = pl.ds(pl.multiple_of((1 - core) * half_rows, half_rows), half_rows)

    def others(body):
        def step_body(step, carry):
            body(lax.rem(chip + step, chips))
            return carry

        lax.fori_loop(1, chips, step_body, 0)

    def reduce_copies(pair_kind, kind, away, near, send, recv):
        def pair_copy(target, source):
            return remote(pair_kind, away, near, target, source)

        def copy(target_chip, source_chip):
            return remote(
                kind,
                send.at[target_chip],
                recv.at[source_chip],
                target_chip * 2 + core,
                source_chip * 2 + core,
            )

        return pair_copy, copy

    def reduce_to_owners(copies, away, near, send, recv):
        pair_copy, copy = copies
        away[...] = stage[away_half, :].astype(BF16).reshape(away.shape)
        pair_copy(sibling, me).start()
        pair_copy(me, sibling).wait_recv()
        total = stage[own_half, :].reshape(near.shape) + near[...].astype(F32)
        send[...] = total.astype(BF16)
        others(lambda other: copy(other, chip).start())
        recv[chip] = send[chip]

    proj_refs = (proj_away, proj_near, proj_send, proj_recv)
    proj_copies = reduce_copies(PROJ_PAIR, PROJ, *proj_refs)
    reduce_to_owners(proj_copies, *proj_refs)
    others(lambda other: proj_copies[1](chip, other).wait_recv())
    state = res_wide[...] + jnp.sum(proj_recv[...].astype(F32), axis=0)
    state = state.reshape(rows_dev, chunks, LANES)
    squares = jnp.sum(jnp.sum(state * state, axis=1, keepdims=True), axis=2, keepdims=True)
    normed = state * lax.rsqrt(squares / width + epsilon) * gain_wide[...][None]
    normed = normed.reshape(rows_dev * chunks, LANES)
    row_send[...] = normed.astype(BF16)

    def row_copy(target, source_chip):
        source = source_chip * 2 + core
        return remote(ROWS, row_send, row_recv.at[core * chips + source_chip], target, source)

    def row_pair_copy(target, source, at):
        block = row_recv.at[at]
        return pltpu.make_async_remote_copy(
            src_ref=block,
            dst_ref=block,
            send_sem=send_sem.at[ROWS_PAIR, at],
            recv_sem=recv_sem.at[ROWS_PAIR, at],
            device_id={"ctx": target},
            device_id_type=MESH,
        )

    others(lambda other: row_copy(other * 2 + core, chip).start())
    row_recv[core * chips + chip] = row_send[...]
    row_pair_copy(sibling, me, core * chips + chip).start()

    def hand_on(other):
        row_copy(me, other).wait_recv()
        row_pair_copy(sibling, me, core * chips + other).start()

    others(hand_on)

    def handed(at, carry):
        row_pair_copy(me, sibling, (1 - core) * chips + at).wait_recv()
        return carry

    lax.fori_loop(0, chips, handed, 0)
    stage[...] = row_recv[...].astype(F32).reshape(stage.shape)
    for c in range(chunks):
        x_all[:, c * LANES : (c + 1) * LANES] = stage[
            pl.ds(c, n_rows, stride=chunks), :
        ].astype(BF16)

    loads[3].wait()
    loads[4].wait()
    hidden = act.shape[1]
    step_cols = 2 * LANES if hidden % (2 * LANES) == 0 else LANES
    for at in range(hidden // step_cols):
        lanes = slice(at * step_cols, (at + 1) * step_cols)
        gate = jnp.dot(x_all[...], wg[:, lanes], preferred_element_type=F32)
        up = jnp.dot(x_all[...], wu[:, lanes], preferred_element_type=F32)
        act[:, lanes] = (gate / (1.0 + jnp.exp(-gate)) * up).astype(BF16)
    loads[5].wait()
    for at in range(width // wide):
        tile = jnp.dot(act[...], wd[:, at * wide : (at + 1) * wide], preferred_element_type=F32)
        spread(4 * at, tile * jnp.concatenate([mix[...]] * 4, axis=1))
    back_refs = (back_away, back_near, back_send, back_recv)
    back_copies = reduce_copies(BACK_PAIR, BACK, *back_refs)
    reduce_to_owners(back_copies, *back_refs)

    for step in range(1, team):
        for copy in key_copies(*near(step), mate):
            copy.wait_send()
    for at in range(team):
        target = mate * team + at

        @pl.when(target != me)
        def _():
            for copy in head_copies(target, at, me, plane):
                copy.wait_send()

    peers(lambda other: q_copy(other, me).wait_send())
    proj_copies[0](sibling, me).wait_send()
    back_copies[0](sibling, me).wait_send()

    def sent(other):
        proj_copies[1](other, chip).wait_send()
        row_copy(other * 2 + core, chip).wait_send()
        row_pair_copy(sibling, me, core * chips + other).wait_send()

    others(sent)
    row_pair_copy(sibling, me, core * chips + chip).wait_send()
    others(lambda other: back_copies[1](chip, other).wait_recv())
    final = state + jnp.sum(back_recv[...].astype(F32), axis=0).reshape(state.shape)
    for r in range(rows_dev):
        res_wide[r * chunks : (r + 1) * chunks, :] = final[r]
    for c in range(chunks):
        out_ref[:, c * LANES : (c + 1) * LANES] = res_wide[
            pl.ds(c, rows_dev, stride=chunks), :
        ].astype(BF16)
    others(lambda other: back_copies[1](other, chip).wait_send())


def local(*args):
    (queries, cache_keys, _, _, _, _, residual_in, out_weight, _, expert_gate) = args[:10]
    shards = lax.axis_size("ctx")
    rows_dev, width = residual_in.shape
    capacity = max(2, 2 * rows_dev * TOP // shards)
    if not fits(shards, rows_dev, width, capacity, expert_gate.shape[0]):
        return plain(*args)
    team = shards // KV_HEADS
    hidden = expert_gate.shape[2]
    cache = cache_keys.shape[0]
    rows = rows_dev * width // LANES
    any_spec = pl.BlockSpec(memory_space=pl.ANY)
    vmem = pl.BlockSpec(memory_space=pltpu.VMEM)
    smem = pl.BlockSpec(memory_space=pltpu.SMEM)
    blocks = pltpu.VMEM((shards, rows, LANES), BF16)
    halves = pltpu.VMEM((shards // 2, rows, LANES), BF16)
    tiles = pltpu.VMEM((team, LANES, shards * SUB), BF16)
    stats = pltpu.VMEM((team, SUB, LANES), F32)
    keys = pltpu.VMEM((team, cache, LANES), BF16)
    new = pltpu.VMEM((KV_HEADS, 2 * SUB, LANES), BF16)
    flops = 2 * shards * rows_dev * width * (3 * hidden + out_weight.shape[0])
    return pl.pallas_call(
        functools.partial(layer_kernel, shards),
        out_shape=jax.ShapeDtypeStruct((rows_dev, width), BF16),
        in_specs=[any_spec] * 5 + [smem] + [any_spec] * 8,
        out_specs=vmem,
        scratch_shapes=[
            pltpu.VMEM(out_weight.shape, BF16),
            pltpu.VMEM((width, hidden), BF16),
            pltpu.VMEM((width, hidden), BF16),
            pltpu.VMEM((hidden, width), BF16),
            pltpu.VMEM((KV_HEADS, team * SUB, LANES), F32),
            pltpu.VMEM((KV_HEADS, team * SUB, LANES), BF16),
            pltpu.VMEM((shards, team * SUB, LANES), BF16),
            pltpu.VMEM((team, shards * SUB, LANES), BF16),
            keys,
            keys,
            pltpu.VMEM((KV_HEADS, 2 * SUB, LANES), F32),
            new,
            new,
            tiles,
            tiles,
            stats,
            stats,
            pltpu.VMEM((shards * rows, LANES), F32),
            halves,
            halves,
            halves,
            halves,
            pltpu.VMEM((rows, LANES), F32),
            pltpu.VMEM((width // LANES, LANES), F32),
            pltpu.VMEM((shards, LANES), F32),
            pltpu.VMEM((shards * rows_dev, LANES), F32),
            pltpu.VMEM((rows, LANES), BF16),
            blocks,
            pltpu.VMEM((shards * rows_dev, width), BF16),
            pltpu.VMEM((shards * rows_dev, hidden), BF16),
            halves,
            halves,
            halves,
            halves,
            *(pltpu.VMEM(args[i].shape, args[i].dtype) for i in (0, 3, 4, 6)),
            pltpu.VMEM((width,), BF16),
            *(pltpu.VMEM(args[i].shape, args[i].dtype) for i in (12, 13)),
            pltpu.SemaphoreType.DMA((13,)),
            pltpu.SemaphoreType.DMA((KINDS, shards)),
            pltpu.SemaphoreType.DMA((KINDS, shards)),
        ],
        compiler_params=pltpu.CompilerParams(
            collective_id=0, has_side_effects=True, vmem_limit_bytes=60 * 1024 * 1024
        ),
        cost_estimate=pl.CostEstimate(
            flops=flops, bytes_accessed=2 * 3 * hidden * width, transcendentals=0
        ),
    )(*args)


def solution(mesh):
    placed = (
        P(("groups", "ctx"), None),
        P(("groups", "ctx"), None),
        P(("groups", "ctx"), None),
        P(("groups", "ctx"), None),
        P(("groups", "ctx"), None),
        P(("groups", "ctx")),
        P(("groups", "ctx"), None),
        P("ctx", None),
        P(),
        P("ctx", None, None),
        P("ctx", None, None),
        P("ctx", None, None),
        P(("groups", "ctx"), None),
        P(("groups", "ctx"), None),
    )
    return jax.shard_map(
        local, mesh=mesh, in_specs=placed, out_specs=P(("groups", "ctx"), None), check_vma=False
    )
```

```python
import functools

import jax
import jax.numpy as jnp
from jax import lax
from jax.experimental import pallas as pl
from jax.experimental.pallas import tpu as pltpu
from jax.sharding import PartitionSpec as P

HEADS = 32
KV_HEADS = 4
HEAD_DIM = 128
TOP = 8


MASKED = -1e30
epsilon = 1e-06


def plain(
    queries,
    cache_keys,
    cache_values,
    new_keys,
    new_values,
    cache_lengths,
    residual_in,
    out_weight,
    norm_gain,
    expert_gate,
    expert_up,
    expert_down,
    expert_ids,
    expert_weights,
):
    shards = lax.axis_size("ctx")
    device = lax.axis_index("ctx")
    rows_dev = residual_in.shape[0]
    capacity = max(2, 2 * rows_dev * TOP // shards)
    group_size = HEADS // KV_HEADS
    whole_queries = lax.all_gather(queries, "ctx", axis=0, tiled=True)
    all_rows = whole_queries.shape[0]
    query_heads = whole_queries.reshape(all_rows, KV_HEADS, group_size, HEAD_DIM)
    local_cache = cache_keys.shape[0]
    key_rows = jnp.concatenate([cache_keys, new_keys], 0).reshape(
        local_cache + rows_dev, KV_HEADS, HEAD_DIM
    )
    value_rows = jnp.concatenate([cache_values, new_values], 0).reshape(
        local_cache + rows_dev, KV_HEADS, HEAD_DIM
    )
    slot_ids = jnp.arange(local_cache + rows_dev, dtype=jnp.int32)
    span_pos = device * rows_dev + slot_ids - local_cache
    row_ids = jnp.arange(all_rows, dtype=jnp.int32)
    usable = jnp.where(
        slot_ids[None, :] < local_cache,
        (slot_ids < cache_lengths[0])[None, :],
        span_pos[None, :] <= row_ids[:, None],
    )
    scores = jnp.einsum(
        "rkgd,nkd->kgrn", query_heads, key_rows, preferred_element_type=jnp.float32
    ) * HEAD_DIM ** (-0.5)
    scores = jnp.where(usable, scores, MASKED)
    maxima = jnp.max(scores, axis=-1)
    exp_weights = jnp.where(usable, jnp.exp(scores - maxima[..., None]), 0.0)
    totals = jnp.sum(exp_weights, axis=-1)
    numerators = jnp.einsum(
        "kgrn,nkd->rkgd",
        exp_weights.astype(jnp.bfloat16),
        value_rows,
        preferred_element_type=jnp.float32,
    ).reshape(all_rows, HEADS, HEAD_DIM)
    maxima = maxima.transpose(2, 0, 1).reshape(all_rows, HEADS)
    totals = totals.transpose(2, 0, 1).reshape(all_rows, HEADS)
    largest = lax.pmax(maxima, "ctx")
    rescale = jnp.exp(maxima - largest)
    denoms = lax.psum(totals * rescale, "ctx")
    weighted = (numerators * (rescale / denoms)[..., None]).reshape(all_rows, HEADS * HEAD_DIM)
    columns = lax.psum_scatter(weighted, "ctx", scatter_dimension=1, tiled=True).astype(
        jnp.bfloat16
    )
    projected = lax.psum_scatter(
        jnp.dot(columns, out_weight, preferred_element_type=jnp.float32),
        "ctx",
        scatter_dimension=0,
        tiled=True,
    )
    state = residual_in.astype(jnp.float32) + projected
    normed = (
        state
        * lax.rsqrt(jnp.mean(state * state, axis=1, keepdims=True) + epsilon)
        * norm_gain.astype(jnp.float32)
    ).astype(jnp.bfloat16)
    n_slots = shards * capacity
    flat_ids = expert_ids.reshape(-1)
    places = jnp.arange(flat_ids.shape[0], dtype=jnp.int32)
    earlier = (flat_ids[:, None] == flat_ids[None, :]) & (places[None, :] < places[:, None])
    slot_of = flat_ids * capacity + jnp.sum(earlier.astype(jnp.int32), axis=1)
    one_hot = (slot_of[:, None] == jnp.arange(n_slots, dtype=jnp.int32)[None, :]).astype(
        jnp.float32
    )
    dispatch_map = one_hot.reshape(rows_dev, TOP, n_slots).sum(1)
    outgoing = (
        jnp.dot(dispatch_map.T.astype(jnp.bfloat16), normed, preferred_element_type=jnp.float32)
        .astype(jnp.bfloat16)
        .reshape(shards, capacity, normed.shape[1])
    )
    received = lax.all_to_all(outgoing, "ctx", split_axis=0, concat_axis=0, tiled=True)
    gate_out = jnp.einsum(
        "scd,df->scf", received, expert_gate[0], preferred_element_type=jnp.float32
    )
    up_out = jnp.einsum("scd,df->scf", received, expert_up[0], preferred_element_type=jnp.float32)
    activated = (jax.nn.silu(gate_out) * up_out).astype(jnp.bfloat16)
    expert_out = jnp.einsum(
        "scf,fd->scd", activated, expert_down[0], preferred_element_type=jnp.float32
    ).astype(jnp.bfloat16)
    back = lax.all_to_all(expert_out, "ctx", split_axis=0, concat_axis=0, tiled=True)
    combine_map = (
        (one_hot * expert_weights.reshape(-1)[:, None]).reshape(rows_dev, TOP, n_slots).sum(1)
    )
    expert_sum = jnp.dot(
        combine_map,
        back.reshape(n_slots, normed.shape[1]).astype(jnp.float32),
        precision=lax.Precision.HIGHEST,
    )
    return (state + expert_sum).astype(jnp.bfloat16)


LANES = 128
SUB = 8
MESH = pl.DeviceIdType.MESH
F32 = jnp.float32
BF16 = jnp.bfloat16
Q, K, V, NEW, NUM, STAT, PROJ, ROWS, BACK = range(9)


def fits(shards, rows_dev, width, capacity, experts_dev):
    team = shards // KV_HEADS
    if shards % KV_HEADS or team == 0 or (HEADS // KV_HEADS) % team:
        return False
    pair = HEADS // KV_HEADS // team
    return (
        experts_dev == 1
        and team == KV_HEADS
        and HEAD_DIM == LANES
        and shards * SUB == LANES
        and (shards * rows_dev) % (2 * SUB) == 0
        and pair * rows_dev <= SUB
        and capacity >= rows_dev
        and width % (2 * SUB * LANES) == 0
    )


def layer_kernel(
    shards,
    q_hbm,
    ck_ref,
    cv_ref,
    nk_hbm,
    nv_hbm,
    len_ref,
    res_hbm,
    wo_ref,
    gain_hbm,
    wg_ref,
    wu_ref,
    wd_ref,
    ids_hbm,
    ew_hbm,
    out_ref,
    wo,
    wg,
    wu,
    wd,
    q_wide,
    q_send,
    q_recv,
    q_heads,
    k_all,
    v_all,
    new_wide,
    new_send,
    new_recv,
    num_send,
    num_recv,
    stat_send,
    stat_recv,
    stage,
    proj_send,
    proj_recv,
    res_wide,
    gain_wide,
    mix,
    row_send,
    row_recv,
    x_all,
    act,
    back_send,
    back_recv,
    q_ref,
    nk_ref,
    nv_ref,
    res_ref,
    gain_ref,
    ids_ref,
    ew_ref,
    load_sem,
    send_sem,
    recv_sem,
    send_all,
    recv_all,
):
    me = lax.axis_index("ctx")
    team = shards // KV_HEADS
    pair = HEADS // KV_HEADS // team
    rows_dev, width = res_hbm.shape
    chunks = width // LANES
    cache = ck_ref.shape[0]
    plane, mate = me // team, me % team

    barrier = pltpu.get_barrier_semaphore()

    def greet(step, carry):
        pl.semaphore_signal(
            barrier, inc=1, device_id={"ctx": lax.rem(me + step, shards)}, device_id_type=MESH
        )
        return carry

    lax.fori_loop(1, shards, greet, 0)

    own_lanes = pl.ds(pl.multiple_of(mate * LANES, LANES), LANES)
    small = [
        (q_hbm, q_ref),
        (nk_hbm, nk_ref),
        (nv_hbm, nv_ref),
        (res_hbm, res_ref),
        (gain_hbm, gain_ref),
        (ids_hbm, ids_ref),
        (ew_hbm, ew_ref),
    ]
    large = [
        (ck_ref.at[:, own_lanes], k_all.at[mate]),
        (cv_ref.at[:, own_lanes], v_all.at[mate]),
        (wo_ref, wo),
        (wg_ref.at[0], wg),
        (wu_ref.at[0], wu),
        (wd_ref.at[0], wd),
    ]
    loads = [
        pltpu.make_async_copy(src, dst, load_sem.at[i])
        for i, (src, dst) in enumerate(small + large)
    ]
    early = len(small) + 2
    for load in loads[:early]:
        load.start()
    for load in loads[: len(small)]:
        load.wait()

    q_wide[...] = jnp.zeros_like(q_wide)
    for one in range(HEADS):
        kv, rest = divmod(one, HEADS // KV_HEADS)
        who, which = divmod(rest, pair)
        q_wide[kv, pl.ds(who * SUB + which * rows_dev, rows_dev), :] = q_ref[
            :, one * LANES : (one + 1) * LANES
        ].astype(F32)
    q_send[...] = q_wide[...].astype(BF16)
    new_wide[...] = jnp.zeros_like(new_wide)
    live = jnp.full((1, LANES), len_ref[0], jnp.int32).astype(F32)
    for kv in range(KV_HEADS):
        lanes = slice(kv * LANES, (kv + 1) * LANES)
        new_wide[kv, 0:rows_dev, :] = nk_ref[:, lanes].astype(F32)
        new_wide[kv, rows_dev : rows_dev + 1, :] = live
        new_wide[kv, SUB : SUB + rows_dev, :] = nv_ref[:, lanes].astype(F32)
    new_send[...] = new_wide[...].astype(BF16)

    def remote(kind, src, dst, target, source):
        return pltpu.make_async_remote_copy(
            src_ref=src,
            dst_ref=dst,
            send_sem=send_sem.at[kind, target],
            recv_sem=recv_sem.at[kind, source],
            device_id={"ctx": target},
            device_id_type=MESH,
        )

    def near(step):
        other = lax.rem(mate + step, team)
        return other, plane * team + other

    def key_copies(lane_head, target, source_mate):
        lanes = pl.ds(pl.multiple_of(lane_head * LANES, LANES), LANES)
        source = plane * team + source_mate
        return (
            remote(K, ck_ref.at[:, lanes], k_all.at[source_mate], target, source),
            remote(V, cv_ref.at[:, lanes], v_all.at[source_mate], target, source),
            remote(NEW, new_send.at[lane_head], new_recv.at[source_mate], target, source),
        )

    pl.semaphore_wait(barrier, shards - 1)

    def peers(body):
        def step_body(step, carry):
            side = 2 * (step % 2) - 1
            body(lax.rem(me + shards // 2 + (step + 1) // 2 * side, shards))
            return carry

        lax.fori_loop(0, shards - 1, step_body, 0)

    def all_remote(kind, src, dst, target):
        return pltpu.make_async_remote_copy(
            src_ref=src,
            dst_ref=dst,
            send_sem=send_all.at[kind],
            recv_sem=recv_all.at[kind],
            device_id={"ctx": target},
            device_id_type=MESH,
        )

    def wait_all(sem, kind, ref):
        most = ref.at[pl.ds(0, shards - 1)]
        pltpu.make_async_copy(most, most, sem.at[kind]).wait()

    def q_copy(target, source):
        return all_remote(Q, q_send.at[target % team], q_recv.at[source], target)

    peers(lambda other: q_copy(other, me).start())
    for step in range(1, team):
        for copy in key_copies(*near(step), mate):
            copy.start()
    for load in loads[early:]:
        load.start()
    loads = loads[len(small) :]

    q_recv[me] = q_send[mate]
    new_recv[mate] = new_send[mate]

    for c in range(chunks):
        lanes = slice(c * LANES, (c + 1) * LANES)
        res_wide[pl.ds(c, rows_dev, stride=chunks), :] = res_ref[:, lanes].astype(F32)
        gain_wide[c : c + 1, :] = gain_ref[lanes].astype(F32).reshape(1, LANES)
    for e in range(shards):
        share = jnp.where(ids_ref[...] == e, ew_ref[...], 0.0)
        mix[e, 0:rows_dev, :] = jnp.broadcast_to(
            jnp.sum(share, axis=1, keepdims=True), (rows_dev, LANES)
        )

    wait_all(recv_all, Q, q_recv)
    gathered = q_recv[...].astype(F32).reshape(shards, team, SUB, LANES)
    for one in range(team):
        q_heads[one] = gathered[:, one].reshape(shards * SUB, LANES).astype(BF16)
    loads[0].wait()
    loads[1].wait()
    for step in range(1, team):
        other, _ = near(step)
        for copy in key_copies(mate, me, other):
            copy.wait_recv()

    n_cache = team * cache
    n_new = team * SUB
    fresh = new_recv[...].astype(F32)
    new_k = fresh[:, 0:SUB].reshape(n_new, LANES).astype(BF16)
    new_v = fresh[:, SUB : 2 * SUB].reshape(n_new, LANES).astype(BF16)
    lengths = fresh[:, rows_dev : rows_dev + 1, :]
    spot = lax.broadcasted_iota(jnp.int32, (team, cache, LANES), 1).astype(F32)
    cache_ok = (spot < lengths).reshape(n_cache, LANES)
    lane = lax.broadcasted_iota(jnp.int32, (n_new, LANES), 1)
    place = lax.broadcasted_iota(jnp.int32, (n_new, LANES), 0)
    row_of = (lane // SUB) * rows_dev + (lane % SUB) % rows_dev
    key_at = place % SUB
    span = (plane * team + place // SUB) * rows_dev + key_at
    new_ok = (key_at < rows_dev) & (span <= row_of)
    across = (((1,), (1,)), ((), ()))
    down = (((0,), (0,)), ((), ()))
    scale = HEAD_DIM ** (-0.5)
    stat_row = lax.broadcasted_iota(jnp.int32, (SUB, LANES), 0)

    def head_copies(target, target_mate, source, source_plane):
        return (
            remote(NUM, num_send.at[target_mate], num_recv.at[source_plane], target, source),
            remote(STAT, stat_send.at[target_mate], stat_recv.at[source_plane], target, source),
        )

    def attend(step, carry):
        to = lax.rem(plane + step, team)
        queries = q_heads[to]
        keys = k_all[...].reshape(n_cache, LANES)
        old = lax.dot_general(keys, queries, across, preferred_element_type=F32) * scale
        new = lax.dot_general(new_k, queries, across, preferred_element_type=F32) * scale
        old = jnp.where(cache_ok, old, MASKED)
        new = jnp.where(new_ok, new, MASKED)
        top = jnp.maximum(
            jnp.max(old, axis=0, keepdims=True), jnp.max(new, axis=0, keepdims=True)
        )
        old = jnp.where(cache_ok, jnp.exp(old - top), 0.0)
        new = jnp.where(new_ok, jnp.exp(new - top), 0.0)
        total = jnp.sum(old, axis=0, keepdims=True) + jnp.sum(new, axis=0, keepdims=True)
        values = v_all[...].reshape(n_cache, LANES)
        numer = lax.dot_general(values, old.astype(BF16), down, preferred_element_type=F32)
        numer += lax.dot_general(new_v, new.astype(BF16), down, preferred_element_type=F32)
        num_send[to] = numer.astype(BF16)
        stat_send[to] = jnp.where(stat_row == 0, top, total)

        target = mate * team + to

        @pl.when(target != me)
        def _():
            for copy in head_copies(target, to, me, plane):
                copy.start()

        @pl.when(target == me)
        def _():
            num_recv[plane] = num_send[to]
            stat_recv[plane] = stat_send[to]

        return carry

    lax.fori_loop(0, team, attend, 0)
    for at in range(team):
        source = at * team + plane

        @pl.when(source != me)
        def _():
            for copy in head_copies(me, mate, source, at):
                copy.wait_recv()

    tops = stat_recv[:, 0:1, :]
    weight = jnp.exp(tops - jnp.max(tops, axis=0, keepdims=True))
    weight = weight / jnp.sum(weight * stat_recv[:, 1:2, :], axis=0, keepdims=True)
    attention = jnp.sum(num_recv[...].astype(F32) * weight, axis=0).astype(BF16)

    n_rows = shards * rows_dev
    tile_row = lax.broadcasted_iota(jnp.int32, (n_rows, LANES), 0)
    tile_lane = lax.broadcasted_iota(jnp.int32, (n_rows, LANES), 1)
    parts = []
    for which in range(pair):
        pick = (tile_row // rows_dev == tile_lane // SUB) & (
            tile_lane % SUB == which * rows_dev + tile_row % rows_dev
        )
        pick = jnp.where(pick, 1.0, 0.0).astype(BF16)
        parts.append(
            lax.dot_general(pick, attention, across, preferred_element_type=F32).astype(BF16)
        )
    columns = jnp.concatenate(parts, axis=1)

    def spread(first, tile):
        for j in range(tile.shape[1] // LANES):
            stage[pl.ds(first + j, n_rows, stride=chunks), :] = tile[
                :, j * LANES : (j + 1) * LANES
            ]

    loads[2].wait()
    wide = 4 * LANES
    for at in range(width // wide):
        tile = jnp.dot(columns, wo[:, at * wide : (at + 1) * wide], preferred_element_type=F32)
        spread(4 * at, tile)
    proj_send[...] = stage[...].reshape(proj_send.shape).astype(BF16)

    def proj_copy(target, source):
        return all_remote(PROJ, proj_send.at[target], proj_recv.at[source], target)

    peers(lambda other: proj_copy(other, me).start())
    proj_recv[me] = proj_send[me]
    wait_all(recv_all, PROJ, proj_recv)
    state = res_wide[...] + jnp.sum(proj_recv[...].astype(F32), axis=0)
    state = state.reshape(rows_dev, chunks, LANES)
    squares = jnp.sum(jnp.sum(state * state, axis=1, keepdims=True), axis=2, keepdims=True)
    normed = state * lax.rsqrt(squares / width + epsilon) * gain_wide[...][None]
    normed = normed.reshape(rows_dev * chunks, LANES)
    row_send[...] = normed.astype(BF16)

    def row_copy(target, source):
        return all_remote(ROWS, row_send, row_recv.at[source], target)

    peers(lambda other: row_copy(other, me).start())
    row_recv[me] = row_send[...]
    wait_all(recv_all, ROWS, row_recv)

    stage[...] = row_recv[...].astype(F32).reshape(stage.shape)
    for c in range(chunks):
        x_all[:, c * LANES : (c + 1) * LANES] = stage[
            pl.ds(c, n_rows, stride=chunks), :
        ].astype(BF16)

    loads[3].wait()
    loads[4].wait()
    hidden = act.shape[1]
    step_cols = 2 * LANES if hidden % (2 * LANES) == 0 else LANES
    for at in range(hidden // step_cols):
        lanes = slice(at * step_cols, (at + 1) * step_cols)
        gate = jnp.dot(x_all[...], wg[:, lanes], preferred_element_type=F32)
        up = jnp.dot(x_all[...], wu[:, lanes], preferred_element_type=F32)
        act[:, lanes] = (gate / (1.0 + jnp.exp(-gate)) * up).astype(BF16)
    loads[5].wait()
    for at in range(width // wide):
        tile = jnp.dot(act[...], wd[:, at * wide : (at + 1) * wide], preferred_element_type=F32)
        spread(4 * at, tile)
    back_send[...] = stage[...].reshape(back_send.shape).astype(BF16)

    def back_copy(target, source):
        return all_remote(BACK, back_send.at[target], back_recv.at[source], target)

    peers(lambda other: back_copy(other, me).start())
    back_recv[me] = back_send[me]

    for step in range(1, team):
        for copy in key_copies(*near(step), mate):
            copy.wait_send()
    for at in range(team):
        target = mate * team + at

        @pl.when(target != me)
        def _():
            for copy in head_copies(target, at, me, plane):
                copy.wait_send()

    wait_all(send_all, Q, q_recv)
    wait_all(send_all, PROJ, proj_recv)
    wait_all(send_all, ROWS, row_recv)
    wait_all(recv_all, BACK, back_recv)

    def combine(e, total):
        block = back_recv[e].astype(F32).reshape(rows_dev, chunks, LANES)
        share = mix[e]
        return tuple(total[r] + share[r : r + 1, :] * block[r] for r in range(rows_dev))

    final = lax.fori_loop(0, shards, combine, tuple(state[r] for r in range(rows_dev)))
    for r in range(rows_dev):
        res_wide[r * chunks : (r + 1) * chunks, :] = final[r]
    for c in range(chunks):
        out_ref[:, c * LANES : (c + 1) * LANES] = res_wide[
            pl.ds(c, rows_dev, stride=chunks), :
        ].astype(BF16)
    wait_all(send_all, BACK, back_recv)


def local(*args):
    (queries, cache_keys, _, _, _, _, residual_in, out_weight, _, expert_gate) = args[:10]
    shards = lax.axis_size("ctx")
    rows_dev, width = residual_in.shape
    capacity = max(2, 2 * rows_dev * TOP // shards)
    if not fits(shards, rows_dev, width, capacity, expert_gate.shape[0]):
        return plain(*args)
    team = shards // KV_HEADS
    hidden = expert_gate.shape[2]
    cache = cache_keys.shape[0]
    rows = rows_dev * width // LANES
    any_spec = pl.BlockSpec(memory_space=pl.ANY)
    vmem = pl.BlockSpec(memory_space=pltpu.VMEM)
    smem = pl.BlockSpec(memory_space=pltpu.SMEM)
    blocks = pltpu.VMEM((shards, rows, LANES), BF16)
    tiles = pltpu.VMEM((team, LANES, shards * SUB), BF16)
    stats = pltpu.VMEM((team, SUB, LANES), F32)
    keys = pltpu.VMEM((team, cache, LANES), BF16)
    new = pltpu.VMEM((KV_HEADS, 2 * SUB, LANES), BF16)
    flops = 2 * shards * rows_dev * width * (3 * hidden + out_weight.shape[0])
    return pl.pallas_call(
        functools.partial(layer_kernel, shards),
        out_shape=jax.ShapeDtypeStruct((rows_dev, width), BF16),
        in_specs=[any_spec] * 5 + [smem] + [any_spec] * 8,
        out_specs=vmem,
        scratch_shapes=[
            pltpu.VMEM(out_weight.shape, BF16),
            pltpu.VMEM((width, hidden), BF16),
            pltpu.VMEM((width, hidden), BF16),
            pltpu.VMEM((hidden, width), BF16),
            pltpu.VMEM((KV_HEADS, team * SUB, LANES), F32),
            pltpu.VMEM((KV_HEADS, team * SUB, LANES), BF16),
            pltpu.VMEM((shards, team * SUB, LANES), BF16),
            pltpu.VMEM((team, shards * SUB, LANES), BF16),
            keys,
            keys,
            pltpu.VMEM((KV_HEADS, 2 * SUB, LANES), F32),
            new,
            new,
            tiles,
            tiles,
            stats,
            stats,
            pltpu.VMEM((shards * rows, LANES), F32),
            blocks,
            blocks,
            pltpu.VMEM((rows, LANES), F32),
            pltpu.VMEM((width // LANES, LANES), F32),
            pltpu.VMEM((shards, SUB, LANES), F32),
            pltpu.VMEM((rows, LANES), BF16),
            blocks,
            pltpu.VMEM((shards * rows_dev, width), BF16),
            pltpu.VMEM((shards * rows_dev, hidden), BF16),
            blocks,
            blocks,
            *(pltpu.VMEM(args[i].shape, args[i].dtype) for i in (0, 3, 4, 6)),
            pltpu.VMEM((width,), BF16),
            *(pltpu.VMEM(args[i].shape, args[i].dtype) for i in (12, 13)),
            pltpu.SemaphoreType.DMA((13,)),
            pltpu.SemaphoreType.DMA((9, shards)),
            pltpu.SemaphoreType.DMA((9, shards)),
            pltpu.SemaphoreType.DMA((9,)),
            pltpu.SemaphoreType.DMA((9,)),
        ],
        compiler_params=pltpu.CompilerParams(
            collective_id=0, has_side_effects=True, vmem_limit_bytes=60 * 1024 * 1024
        ),
        cost_estimate=pl.CostEstimate(
            flops=flops, bytes_accessed=2 * 3 * hidden * width, transcendentals=0
        ),
    )(*args)


def solution(mesh):
    placed = (
        P(("groups", "ctx"), None),
        P(("groups", "ctx"), None),
        P(("groups", "ctx"), None),
        P(("groups", "ctx"), None),
        P(("groups", "ctx"), None),
        P(("groups", "ctx")),
        P(("groups", "ctx"), None),
        P("ctx", None),
        P(),
        P("ctx", None, None),
        P("ctx", None, None),
        P("ctx", None, None),
        P(("groups", "ctx"), None),
        P(("groups", "ctx"), None),
    )
    return jax.shard_map(
        local, mesh=mesh, in_specs=placed, out_specs=P(("groups", "ctx"), None), check_vma=False
    )
```

```python
import functools

import jax
import jax.numpy as jnp
from jax import lax
from jax.experimental import pallas as pl
from jax.experimental.pallas import tpu as pltpu
from jax.sharding import PartitionSpec as P

HEADS = 32
KV_HEADS = 4
HEAD_DIM = 128
TOP = 8


MASKED = -1e30
epsilon = 1e-06


def plain(
    queries,
    cache_keys,
    cache_values,
    new_keys,
    new_values,
    cache_lengths,
    residual_in,
    out_weight,
    norm_gain,
    expert_gate,
    expert_up,
    expert_down,
    expert_ids,
    expert_weights,
):
    shards = lax.axis_size("ctx")
    device = lax.axis_index("ctx")
    rows_dev = residual_in.shape[0]
    capacity = max(2, 2 * rows_dev * TOP // shards)
    group_size = HEADS // KV_HEADS
    whole_queries = lax.all_gather(queries, "ctx", axis=0, tiled=True)
    all_rows = whole_queries.shape[0]
    query_heads = whole_queries.reshape(all_rows, KV_HEADS, group_size, HEAD_DIM)
    local_cache = cache_keys.shape[0]
    key_rows = jnp.concatenate([cache_keys, new_keys], 0).reshape(
        local_cache + rows_dev, KV_HEADS, HEAD_DIM
    )
    value_rows = jnp.concatenate([cache_values, new_values], 0).reshape(
        local_cache + rows_dev, KV_HEADS, HEAD_DIM
    )
    slot_ids = jnp.arange(local_cache + rows_dev, dtype=jnp.int32)
    span_pos = device * rows_dev + slot_ids - local_cache
    row_ids = jnp.arange(all_rows, dtype=jnp.int32)
    usable = jnp.where(
        slot_ids[None, :] < local_cache,
        (slot_ids < cache_lengths[0])[None, :],
        span_pos[None, :] <= row_ids[:, None],
    )
    scores = jnp.einsum(
        "rkgd,nkd->kgrn", query_heads, key_rows, preferred_element_type=jnp.float32
    ) * HEAD_DIM ** (-0.5)
    scores = jnp.where(usable, scores, MASKED)
    maxima = jnp.max(scores, axis=-1)
    exp_weights = jnp.where(usable, jnp.exp(scores - maxima[..., None]), 0.0)
    totals = jnp.sum(exp_weights, axis=-1)
    numerators = jnp.einsum(
        "kgrn,nkd->rkgd",
        exp_weights.astype(jnp.bfloat16),
        value_rows,
        preferred_element_type=jnp.float32,
    ).reshape(all_rows, HEADS, HEAD_DIM)
    maxima = maxima.transpose(2, 0, 1).reshape(all_rows, HEADS)
    totals = totals.transpose(2, 0, 1).reshape(all_rows, HEADS)
    largest = lax.pmax(maxima, "ctx")
    rescale = jnp.exp(maxima - largest)
    denoms = lax.psum(totals * rescale, "ctx")
    weighted = (numerators * (rescale / denoms)[..., None]).reshape(all_rows, HEADS * HEAD_DIM)
    columns = lax.psum_scatter(weighted, "ctx", scatter_dimension=1, tiled=True).astype(
        jnp.bfloat16
    )
    projected = lax.psum_scatter(
        jnp.dot(columns, out_weight, preferred_element_type=jnp.float32),
        "ctx",
        scatter_dimension=0,
        tiled=True,
    )
    state = residual_in.astype(jnp.float32) + projected
    normed = (
        state
        * lax.rsqrt(jnp.mean(state * state, axis=1, keepdims=True) + epsilon)
        * norm_gain.astype(jnp.float32)
    ).astype(jnp.bfloat16)
    n_slots = shards * capacity
    flat_ids = expert_ids.reshape(-1)
    places = jnp.arange(flat_ids.shape[0], dtype=jnp.int32)
    earlier = (flat_ids[:, None] == flat_ids[None, :]) & (places[None, :] < places[:, None])
    slot_of = flat_ids * capacity + jnp.sum(earlier.astype(jnp.int32), axis=1)
    one_hot = (slot_of[:, None] == jnp.arange(n_slots, dtype=jnp.int32)[None, :]).astype(
        jnp.float32
    )
    dispatch_map = one_hot.reshape(rows_dev, TOP, n_slots).sum(1)
    outgoing = (
        jnp.dot(dispatch_map.T.astype(jnp.bfloat16), normed, preferred_element_type=jnp.float32)
        .astype(jnp.bfloat16)
        .reshape(shards, capacity, normed.shape[1])
    )
    received = lax.all_to_all(outgoing, "ctx", split_axis=0, concat_axis=0, tiled=True)
    gate_out = jnp.einsum(
        "scd,df->scf", received, expert_gate[0], preferred_element_type=jnp.float32
    )
    up_out = jnp.einsum("scd,df->scf", received, expert_up[0], preferred_element_type=jnp.float32)
    activated = (jax.nn.silu(gate_out) * up_out).astype(jnp.bfloat16)
    expert_out = jnp.einsum(
        "scf,fd->scd", activated, expert_down[0], preferred_element_type=jnp.float32
    ).astype(jnp.bfloat16)
    back = lax.all_to_all(expert_out, "ctx", split_axis=0, concat_axis=0, tiled=True)
    combine_map = (
        (one_hot * expert_weights.reshape(-1)[:, None]).reshape(rows_dev, TOP, n_slots).sum(1)
    )
    expert_sum = jnp.dot(
        combine_map,
        back.reshape(n_slots, normed.shape[1]).astype(jnp.float32),
        precision=lax.Precision.HIGHEST,
    )
    return (state + expert_sum).astype(jnp.bfloat16)


LANES = 128
SUB = 8
MESH = pl.DeviceIdType.MESH
F32 = jnp.float32
BF16 = jnp.bfloat16
Q, K, V, NEW, NUM, STAT, PROJ, ROWS, BACK, PROJ_PAIR, ROWS_PAIR, BACK_PAIR = range(12)
KINDS = 12


def shuffled(team, i):
    return (i % 2) * (team // 2) + i // 2


def fits(shards, rows_dev, width, capacity, experts_dev):
    team = shards // KV_HEADS
    if shards % KV_HEADS or team == 0 or (HEADS // KV_HEADS) % team:
        return False
    pair = HEADS // KV_HEADS // team
    return (
        experts_dev == 1
        and team == KV_HEADS
        and team % 2 == 0
        and all(shuffled(team, shuffled(team, i)) == i for i in range(team))
        and HEAD_DIM == LANES
        and shards * SUB == LANES
        and (shards * rows_dev) % (2 * SUB) == 0
        and pair * rows_dev <= SUB - 2
        and rows_dev <= team
        and shards <= LANES
        and capacity >= rows_dev
        and width % (2 * SUB * LANES) == 0
    )


def layer_kernel(
    shards,
    q_hbm,
    ck_ref,
    cv_ref,
    nk_hbm,
    nv_hbm,
    len_ref,
    res_hbm,
    wo_ref,
    gain_hbm,
    wg_ref,
    wu_ref,
    wd_ref,
    ids_hbm,
    ew_hbm,
    out_ref,
    wo,
    wg,
    wu,
    wd,
    q_wide,
    q_send,
    q_recv,
    q_heads,
    k_all,
    v_all,
    new_wide,
    new_send,
    new_recv,
    num_send,
    num_recv,
    stat_send,
    stat_recv,
    stage,
    proj_away,
    proj_near,
    proj_send,
    proj_recv,
    res_wide,
    gain_wide,
    mix_all,
    mix,
    row_send,
    row_recv,
    x_all,
    act,
    back_away,
    back_near,
    back_send,
    back_recv,
    q_ref,
    nk_ref,
    nv_ref,
    res_ref,
    gain_ref,
    ids_ref,
    ew_ref,
    load_sem,
    send_sem,
    recv_sem,
):
    me = lax.axis_index("ctx")
    team = shards // KV_HEADS
    pair = HEADS // KV_HEADS // team
    rows_dev, width = res_hbm.shape
    chunks = width // LANES
    cache = ck_ref.shape[0]
    plane, mate = me // team, me % team
    swap = functools.partial(shuffled, team)
    head = swap(mate)
    chips = shards // 2
    chip, core = me // 2, me % 2
    sibling = me + 1 - 2 * core

    barrier = pltpu.get_barrier_semaphore()

    def greet(step, carry):
        pl.semaphore_signal(
            barrier, inc=1, device_id={"ctx": lax.rem(me + step, shards)}, device_id_type=MESH
        )
        return carry

    lax.fori_loop(1, shards, greet, 0)

    own_lanes = pl.ds(pl.multiple_of(head * LANES, LANES), LANES)
    small = [
        (q_hbm, q_ref),
        (nk_hbm, nk_ref),
        (nv_hbm, nv_ref),
        (res_hbm, res_ref),
        (gain_hbm, gain_ref),
        (ids_hbm, ids_ref),
        (ew_hbm, ew_ref),
    ]
    large = [
        (ck_ref.at[:, own_lanes], k_all.at[mate]),
        (cv_ref.at[:, own_lanes], v_all.at[mate]),
        (wo_ref, wo),
        (wg_ref.at[0], wg),
        (wu_ref.at[0], wu),
        (wd_ref.at[0], wd),
    ]
    loads = [
        pltpu.make_async_copy(src, dst, load_sem.at[i])
        for i, (src, dst) in enumerate(small + large)
    ]
    for load in loads:
        load.start()
    for load in loads[: len(small)]:
        load.wait()
    loads = loads[len(small) :]

    q_wide[...] = jnp.zeros_like(q_wide)
    for one in range(HEADS):
        kv, rest = divmod(one, HEADS // KV_HEADS)
        who, which = divmod(rest, pair)
        q_wide[kv, pl.ds(who * SUB + which * rows_dev, rows_dev), :] = q_ref[
            :, one * LANES : (one + 1) * LANES
        ].astype(F32)
    expert = lax.broadcasted_iota(jnp.int32, (rows_dev, LANES), 1)
    routed = jnp.zeros((rows_dev, LANES), F32)
    for k in range(TOP):
        routed += jnp.where(expert == ids_ref[:, k : k + 1], ew_ref[:, k : k + 1], 0.0)
    coarse = routed.astype(BF16).astype(F32)
    fine = routed - coarse
    for kv in range(KV_HEADS):
        for r in range(rows_dev):
            q_wide[kv, (r + 1) * SUB - 2 : (r + 1) * SUB - 1, :] = coarse[r : r + 1]
            q_wide[kv, (r + 1) * SUB - 1 : (r + 1) * SUB, :] = fine[r : r + 1]
    q_send[...] = q_wide[...].astype(BF16)
    new_wide[...] = jnp.zeros_like(new_wide)
    live = jnp.full((1, LANES), len_ref[0], jnp.int32).astype(F32)
    for kv in range(KV_HEADS):
        lanes = slice(kv * LANES, (kv + 1) * LANES)
        new_wide[kv, 0:rows_dev, :] = nk_ref[:, lanes].astype(F32)
        new_wide[kv, rows_dev : rows_dev + 1, :] = live
        new_wide[kv, SUB : SUB + rows_dev, :] = nv_ref[:, lanes].astype(F32)
    new_send[...] = new_wide[...].astype(BF16)

    def remote(kind, src, dst, target, source):
        return pltpu.make_async_remote_copy(
            src_ref=src,
            dst_ref=dst,
            send_sem=send_sem.at[kind, target],
            recv_sem=recv_sem.at[kind, source],
            device_id={"ctx": target},
            device_id_type=MESH,
        )

    def near(step):
        other = lax.rem(mate + step, team)
        return other, plane * team + other

    def key_copies(target_mate, target, source_mate):
        lane_head = swap(target_mate)
        lanes = pl.ds(pl.multiple_of(lane_head * LANES, LANES), LANES)
        source = plane * team + source_mate
        return (
            remote(K, ck_ref.at[:, lanes], k_all.at[source_mate], target, source),
            remote(V, cv_ref.at[:, lanes], v_all.at[source_mate], target, source),
            remote(NEW, new_send.at[lane_head], new_recv.at[source_mate], target, source),
        )

    pl.semaphore_wait(barrier, shards - 1)

    def peers(body):
        def step_body(step, carry):
            body(lax.rem(me + step, shards))
            return carry

        lax.fori_loop(1, shards, step_body, 0)

    def q_copy(target, source):
        return remote(Q, q_send.at[swap(target % team)], q_recv.at[source], target, source)

    peers(lambda other: q_copy(other, me).start())
    for step in range(1, team):
        for copy in key_copies(*near(step), mate):
            copy.start()

    q_recv[me] = q_send[head]
    new_recv[mate] = new_send[head]

    for c in range(chunks):
        lanes = slice(c * LANES, (c + 1) * LANES)
        res_wide[pl.ds(c, rows_dev, stride=chunks), :] = res_ref[:, lanes].astype(F32)
        gain_wide[c : c + 1, :] = gain_ref[lanes].astype(F32).reshape(1, LANES)

    peers(lambda other: q_copy(me, other).wait_recv())
    gathered = q_recv[...].astype(F32).reshape(shards, team, SUB, LANES)
    for one in range(team):
        q_heads[one] = gathered[:, one].reshape(shards * SUB, LANES).astype(BF16)
    at_lane = lax.broadcasted_iota(jnp.int32, (shards, LANES), 1)
    for r in range(rows_dev):
        both = gathered[:, r, SUB - 2, :] + gathered[:, r, SUB - 1, :]
        mine = jnp.sum(jnp.where(at_lane == me, both, 0.0), axis=1, keepdims=True)
        mix_all[...] = jnp.broadcast_to(mine, (shards, LANES))
        for half in range(2):
            mix[pl.ds(half * chips * rows_dev + r, chips, stride=rows_dev), :] = mix_all[
                pl.ds(half, chips, stride=2), :
            ]
    loads[0].wait()
    loads[1].wait()
    for step in range(1, team):
        other, _ = near(step)
        for copy in key_copies(mate, me, other):
            copy.wait_recv()

    n_cache = team * cache
    n_new = team * SUB
    fresh = new_recv[...].astype(F32)
    new_k = fresh[:, 0:SUB].reshape(n_new, LANES).astype(BF16)
    new_v = fresh[:, SUB : 2 * SUB].reshape(n_new, LANES).astype(BF16)
    lengths = fresh[:, rows_dev : rows_dev + 1, :]
    spot = lax.broadcasted_iota(jnp.int32, (team, cache, LANES), 1).astype(F32)
    cache_ok = (spot < lengths).reshape(n_cache, LANES)
    lane = lax.broadcasted_iota(jnp.int32, (n_new, LANES), 1)
    place = lax.broadcasted_iota(jnp.int32, (n_new, LANES), 0)
    row_of = (lane // SUB) * rows_dev + (lane % SUB) % rows_dev
    key_at = place % SUB
    span = (plane * team + place // SUB) * rows_dev + key_at
    new_ok = (key_at < rows_dev) & (span <= row_of)
    across = (((1,), (1,)), ((), ()))
    down = (((0,), (0,)), ((), ()))
    scale = HEAD_DIM ** (-0.5)
    stat_row = lax.broadcasted_iota(jnp.int32, (SUB, LANES), 0)

    def head_copies(target, target_mate, source, source_plane):
        return (
            remote(NUM, num_send.at[target_mate], num_recv.at[source_plane], target, source),
            remote(STAT, stat_send.at[target_mate], stat_recv.at[source_plane], target, source),
        )

    def attend(step, carry):
        to = lax.rem(plane + step, team)
        queries = q_heads[to]
        keys = k_all[...].reshape(n_cache, LANES)
        old = lax.dot_general(keys, queries, across, preferred_element_type=F32) * scale
        new = lax.dot_general(new_k, queries, across, preferred_element_type=F32) * scale
        old = jnp.where(cache_ok, old, MASKED)
        new = jnp.where(new_ok, new, MASKED)
        top = jnp.maximum(
            jnp.max(old, axis=0, keepdims=True), jnp.max(new, axis=0, keepdims=True)
        )
        old = jnp.where(cache_ok, jnp.exp(old - top), 0.0)
        new = jnp.where(new_ok, jnp.exp(new - top), 0.0)
        total = jnp.sum(old, axis=0, keepdims=True) + jnp.sum(new, axis=0, keepdims=True)
        values = v_all[...].reshape(n_cache, LANES)
        numer = lax.dot_general(values, old.astype(BF16), down, preferred_element_type=F32)
        numer += lax.dot_general(new_v, new.astype(BF16), down, preferred_element_type=F32)
        num_send[to] = numer.astype(BF16)
        stat_send[to] = jnp.where(stat_row == 0, top, total)

        target = head * team + to

        @pl.when(target != me)
        def _():
            for copy in head_copies(target, to, me, plane):
                copy.start()

        @pl.when(target == me)
        def _():
            num_recv[plane] = num_send[to]
            stat_recv[plane] = stat_send[to]

        return carry

    lax.fori_loop(0, team, attend, 0)
    for at in range(team):
        source = at * team + swap(plane)

        @pl.when(source != me)
        def _():
            for copy in head_copies(me, mate, source, at):
                copy.wait_recv()

    tops = stat_recv[:, 0:1, :]
    weight = jnp.exp(tops - jnp.max(tops, axis=0, keepdims=True))
    weight = weight / jnp.sum(weight * stat_recv[:, 1:2, :], axis=0, keepdims=True)
    attention = jnp.sum(num_recv[...].astype(F32) * weight, axis=0).astype(BF16)

    n_rows = shards * rows_dev
    tile_row = lax.broadcasted_iota(jnp.int32, (n_rows, LANES), 0)
    tile_lane = lax.broadcasted_iota(jnp.int32, (n_rows, LANES), 1)
    tile_place = tile_row // rows_dev
    tile_device = (tile_place % chips) * 2 + tile_place // chips
    parts = []
    for which in range(pair):
        pick = (tile_device == tile_lane // SUB) & (
            tile_lane % SUB == which * rows_dev + tile_row % rows_dev
        )
        pick = jnp.where(pick, 1.0, 0.0).astype(BF16)
        parts.append(
            lax.dot_general(pick, attention, across, preferred_element_type=F32).astype(BF16)
        )
    columns = jnp.concatenate(parts, axis=1)

    def spread(first, tile):
        for j in range(tile.shape[1] // LANES):
            stage[pl.ds(first + j, n_rows, stride=chunks), :] = tile[
                :, j * LANES : (j + 1) * LANES
            ]

    loads[2].wait()
    wide = 4 * LANES
    for at in range(width // wide):
        tile = jnp.dot(columns, wo[:, at * wide : (at + 1) * wide], preferred_element_type=F32)
        spread(4 * at, tile)

    half_rows = chips * rows_dev * chunks
    own_half = pl.ds(pl.multiple_of(core * half_rows, half_rows), half_rows)
    away_half = pl.ds(pl.multiple_of((1 - core) * half_rows, half_rows), half_rows)

    def others(body):
        def step_body(step, carry):
            body(lax.rem(chip + step, chips))
            return carry

        lax.fori_loop(1, chips, step_body, 0)

    def reduce_copies(pair_kind, kind, away, near, send, recv):
        def pair_copy(target, source):
            return remote(pair_kind, away, near, target, source)

        def copy(target_chip, source_chip):
            return remote(
                kind,
                send.at[target_chip],
                recv.at[source_chip],
                target_chip * 2 + core,
                source_chip * 2 + core,
            )

        return pair_copy, copy

    def reduce_to_owners(copies, away, near, send, recv):
        pair_copy, copy = copies
        away[...] = stage[away_half, :].astype(BF16).reshape(away.shape)
        pair_copy(sibling, me).start()
        pair_copy(me, sibling).wait_recv()
        total = stage[own_half, :].reshape(near.shape) + near[...].astype(F32)
        send[...] = total.astype(BF16)
        others(lambda other: copy(other, chip).start())
        recv[chip] = send[chip]

    proj_refs = (proj_away, proj_near, proj_send, proj_recv)
    proj_copies = reduce_copies(PROJ_PAIR, PROJ, *proj_refs)
    reduce_to_owners(proj_copies, *proj_refs)
    others(lambda other: proj_copies[1](chip, other).wait_recv())
    state = res_wide[...] + jnp.sum(proj_recv[...].astype(F32), axis=0)
    state = state.reshape(rows_dev, chunks, LANES)
    squares = jnp.sum(jnp.sum(state * state, axis=1, keepdims=True), axis=2, keepdims=True)
    normed = state * lax.rsqrt(squares / width + epsilon) * gain_wide[...][None]
    normed = normed.reshape(rows_dev * chunks, LANES)
    row_send[...] = normed.astype(BF16)

    def row_copy(target, source_chip):
        source = source_chip * 2 + core
        return remote(ROWS, row_send, row_recv.at[core * chips + source_chip], target, source)

    def row_pair_copy(target, source, at):
        block = row_recv.at[at]
        return pltpu.make_async_remote_copy(
            src_ref=block,
            dst_ref=block,
            send_sem=send_sem.at[ROWS_PAIR, at],
            recv_sem=recv_sem.at[ROWS_PAIR, at],
            device_id={"ctx": target},
            device_id_type=MESH,
        )

    others(lambda other: row_copy(other * 2 + core, chip).start())
    row_recv[core * chips + chip] = row_send[...]
    row_pair_copy(sibling, me, core * chips + chip).start()

    def hand_on(other):
        row_copy(me, other).wait_recv()
        row_pair_copy(sibling, me, core * chips + other).start()

    others(hand_on)

    def handed(at, carry):
        row_pair_copy(me, sibling, (1 - core) * chips + at).wait_recv()
        return carry

    lax.fori_loop(0, chips, handed, 0)
    stage[...] = row_recv[...].astype(F32).reshape(stage.shape)
    for c in range(chunks):
        x_all[:, c * LANES : (c + 1) * LANES] = stage[
            pl.ds(c, n_rows, stride=chunks), :
        ].astype(BF16)

    loads[3].wait()
    loads[4].wait()
    hidden = act.shape[1]
    step_cols = 2 * LANES if hidden % (2 * LANES) == 0 else LANES
    for at in range(hidden // step_cols):
        lanes = slice(at * step_cols, (at + 1) * step_cols)
        gate = jnp.dot(x_all[...], wg[:, lanes], preferred_element_type=F32)
        up = jnp.dot(x_all[...], wu[:, lanes], preferred_element_type=F32)
        act[:, lanes] = (gate / (1.0 + jnp.exp(-gate)) * up).astype(BF16)
    loads[5].wait()
    for at in range(width // wide):
        tile = jnp.dot(act[...], wd[:, at * wide : (at + 1) * wide], preferred_element_type=F32)
        spread(4 * at, tile * jnp.concatenate([mix[...]] * 4, axis=1))
    back_refs = (back_away, back_near, back_send, back_recv)
    back_copies = reduce_copies(BACK_PAIR, BACK, *back_refs)
    reduce_to_owners(back_copies, *back_refs)

    for step in range(1, team):
        for copy in key_copies(*near(step), mate):
            copy.wait_send()
    for at in range(team):
        target = head * team + at

        @pl.when(target != me)
        def _():
            for copy in head_copies(target, at, me, plane):
                copy.wait_send()

    peers(lambda other: q_copy(other, me).wait_send())
    proj_copies[0](sibling, me).wait_send()
    back_copies[0](sibling, me).wait_send()

    def sent(other):
        proj_copies[1](other, chip).wait_send()
        row_copy(other * 2 + core, chip).wait_send()
        row_pair_copy(sibling, me, core * chips + other).wait_send()

    others(sent)
    row_pair_copy(sibling, me, core * chips + chip).wait_send()
    others(lambda other: back_copies[1](chip, other).wait_recv())
    final = state + jnp.sum(back_recv[...].astype(F32), axis=0).reshape(state.shape)
    for r in range(rows_dev):
        res_wide[r * chunks : (r + 1) * chunks, :] = final[r]
    for c in range(chunks):
        out_ref[:, c * LANES : (c + 1) * LANES] = res_wide[
            pl.ds(c, rows_dev, stride=chunks), :
        ].astype(BF16)
    others(lambda other: back_copies[1](other, chip).wait_send())


def local(*args):
    (queries, cache_keys, _, _, _, _, residual_in, out_weight, _, expert_gate) = args[:10]
    shards = lax.axis_size("ctx")
    rows_dev, width = residual_in.shape
    capacity = max(2, 2 * rows_dev * TOP // shards)
    if not fits(shards, rows_dev, width, capacity, expert_gate.shape[0]):
        return plain(*args)
    team = shards // KV_HEADS
    hidden = expert_gate.shape[2]
    cache = cache_keys.shape[0]
    rows = rows_dev * width // LANES
    any_spec = pl.BlockSpec(memory_space=pl.ANY)
    vmem = pl.BlockSpec(memory_space=pltpu.VMEM)
    smem = pl.BlockSpec(memory_space=pltpu.SMEM)
    blocks = pltpu.VMEM((shards, rows, LANES), BF16)
    halves = pltpu.VMEM((shards // 2, rows, LANES), BF16)
    tiles = pltpu.VMEM((team, LANES, shards * SUB), BF16)
    stats = pltpu.VMEM((team, SUB, LANES), F32)
    keys = pltpu.VMEM((team, cache, LANES), BF16)
    new = pltpu.VMEM((KV_HEADS, 2 * SUB, LANES), BF16)
    flops = 2 * shards * rows_dev * width * (3 * hidden + out_weight.shape[0])
    return pl.pallas_call(
        functools.partial(layer_kernel, shards),
        out_shape=jax.ShapeDtypeStruct((rows_dev, width), BF16),
        in_specs=[any_spec] * 5 + [smem] + [any_spec] * 8,
        out_specs=vmem,
        scratch_shapes=[
            pltpu.VMEM(out_weight.shape, BF16),
            pltpu.VMEM((width, hidden), BF16),
            pltpu.VMEM((width, hidden), BF16),
            pltpu.VMEM((hidden, width), BF16),
            pltpu.VMEM((KV_HEADS, team * SUB, LANES), F32),
            pltpu.VMEM((KV_HEADS, team * SUB, LANES), BF16),
            pltpu.VMEM((shards, team * SUB, LANES), BF16),
            pltpu.VMEM((team, shards * SUB, LANES), BF16),
            keys,
            keys,
            pltpu.VMEM((KV_HEADS, 2 * SUB, LANES), F32),
            new,
            new,
            tiles,
            tiles,
            stats,
            stats,
            pltpu.VMEM((shards * rows, LANES), F32),
            halves,
            halves,
            halves,
            halves,
            pltpu.VMEM((rows, LANES), F32),
            pltpu.VMEM((width // LANES, LANES), F32),
            pltpu.VMEM((shards, LANES), F32),
            pltpu.VMEM((shards * rows_dev, LANES), F32),
            pltpu.VMEM((rows, LANES), BF16),
            blocks,
            pltpu.VMEM((shards * rows_dev, width), BF16),
            pltpu.VMEM((shards * rows_dev, hidden), BF16),
            halves,
            halves,
            halves,
            halves,
            *(pltpu.VMEM(args[i].shape, args[i].dtype) for i in (0, 3, 4, 6)),
            pltpu.VMEM((width,), BF16),
            *(pltpu.VMEM(args[i].shape, args[i].dtype) for i in (12, 13)),
            pltpu.SemaphoreType.DMA((13,)),
            pltpu.SemaphoreType.DMA((KINDS, shards)),
            pltpu.SemaphoreType.DMA((KINDS, shards)),
        ],
        compiler_params=pltpu.CompilerParams(
            collective_id=0, has_side_effects=True, vmem_limit_bytes=60 * 1024 * 1024
        ),
        cost_estimate=pl.CostEstimate(
            flops=flops, bytes_accessed=2 * 3 * hidden * width, transcendentals=0
        ),
    )(*args)


def solution(mesh):
    placed = (
        P(("groups", "ctx"), None),
        P(("groups", "ctx"), None),
        P(("groups", "ctx"), None),
        P(("groups", "ctx"), None),
        P(("groups", "ctx"), None),
        P(("groups", "ctx")),
        P(("groups", "ctx"), None),
        P("ctx", None),
        P(),
        P("ctx", None, None),
        P("ctx", None, None),
        P("ctx", None, None),
        P(("groups", "ctx"), None),
        P(("groups", "ctx"), None),
    )
    return jax.shard_map(
        local, mesh=mesh, in_specs=placed, out_specs=P(("groups", "ctx"), None), check_vma=False
    )
```

```python
import functools

import jax
import jax.numpy as jnp
from jax import lax
from jax.experimental import pallas as pl
from jax.experimental.pallas import tpu as pltpu
from jax.sharding import PartitionSpec as P

HEADS = 32
KV_HEADS = 4
HEAD_DIM = 128
TOP = 8


MASKED = -1e30
epsilon = 1e-06


def plain(
    queries,
    cache_keys,
    cache_values,
    new_keys,
    new_values,
    cache_lengths,
    residual_in,
    out_weight,
    norm_gain,
    expert_gate,
    expert_up,
    expert_down,
    expert_ids,
    expert_weights,
):
    shards = lax.axis_size("ctx")
    device = lax.axis_index("ctx")
    rows_dev = residual_in.shape[0]
    capacity = max(2, 2 * rows_dev * TOP // shards)
    group_size = HEADS // KV_HEADS
    whole_queries = lax.all_gather(queries, "ctx", axis=0, tiled=True)
    all_rows = whole_queries.shape[0]
    query_heads = whole_queries.reshape(all_rows, KV_HEADS, group_size, HEAD_DIM)
    local_cache = cache_keys.shape[0]
    key_rows = jnp.concatenate([cache_keys, new_keys], 0).reshape(
        local_cache + rows_dev, KV_HEADS, HEAD_DIM
    )
    value_rows = jnp.concatenate([cache_values, new_values], 0).reshape(
        local_cache + rows_dev, KV_HEADS, HEAD_DIM
    )
    slot_ids = jnp.arange(local_cache + rows_dev, dtype=jnp.int32)
    span_pos = device * rows_dev + slot_ids - local_cache
    row_ids = jnp.arange(all_rows, dtype=jnp.int32)
    usable = jnp.where(
        slot_ids[None, :] < local_cache,
        (slot_ids < cache_lengths[0])[None, :],
        span_pos[None, :] <= row_ids[:, None],
    )
    scores = jnp.einsum(
        "rkgd,nkd->kgrn", query_heads, key_rows, preferred_element_type=jnp.float32
    ) * HEAD_DIM ** (-0.5)
    scores = jnp.where(usable, scores, MASKED)
    maxima = jnp.max(scores, axis=-1)
    exp_weights = jnp.where(usable, jnp.exp(scores - maxima[..., None]), 0.0)
    totals = jnp.sum(exp_weights, axis=-1)
    numerators = jnp.einsum(
        "kgrn,nkd->rkgd",
        exp_weights.astype(jnp.bfloat16),
        value_rows,
        preferred_element_type=jnp.float32,
    ).reshape(all_rows, HEADS, HEAD_DIM)
    maxima = maxima.transpose(2, 0, 1).reshape(all_rows, HEADS)
    totals = totals.transpose(2, 0, 1).reshape(all_rows, HEADS)
    largest = lax.pmax(maxima, "ctx")
    rescale = jnp.exp(maxima - largest)
    denoms = lax.psum(totals * rescale, "ctx")
    weighted = (numerators * (rescale / denoms)[..., None]).reshape(all_rows, HEADS * HEAD_DIM)
    columns = lax.psum_scatter(weighted, "ctx", scatter_dimension=1, tiled=True).astype(
        jnp.bfloat16
    )
    projected = lax.psum_scatter(
        jnp.dot(columns, out_weight, preferred_element_type=jnp.float32),
        "ctx",
        scatter_dimension=0,
        tiled=True,
    )
    state = residual_in.astype(jnp.float32) + projected
    normed = (
        state
        * lax.rsqrt(jnp.mean(state * state, axis=1, keepdims=True) + epsilon)
        * norm_gain.astype(jnp.float32)
    ).astype(jnp.bfloat16)
    n_slots = shards * capacity
    flat_ids = expert_ids.reshape(-1)
    places = jnp.arange(flat_ids.shape[0], dtype=jnp.int32)
    earlier = (flat_ids[:, None] == flat_ids[None, :]) & (places[None, :] < places[:, None])
    slot_of = flat_ids * capacity + jnp.sum(earlier.astype(jnp.int32), axis=1)
    one_hot = (slot_of[:, None] == jnp.arange(n_slots, dtype=jnp.int32)[None, :]).astype(
        jnp.float32
    )
    dispatch_map = one_hot.reshape(rows_dev, TOP, n_slots).sum(1)
    outgoing = (
        jnp.dot(dispatch_map.T.astype(jnp.bfloat16), normed, preferred_element_type=jnp.float32)
        .astype(jnp.bfloat16)
        .reshape(shards, capacity, normed.shape[1])
    )
    received = lax.all_to_all(outgoing, "ctx", split_axis=0, concat_axis=0, tiled=True)
    gate_out = jnp.einsum(
        "scd,df->scf", received, expert_gate[0], preferred_element_type=jnp.float32
    )
    up_out = jnp.einsum("scd,df->scf", received, expert_up[0], preferred_element_type=jnp.float32)
    activated = (jax.nn.silu(gate_out) * up_out).astype(jnp.bfloat16)
    expert_out = jnp.einsum(
        "scf,fd->scd", activated, expert_down[0], preferred_element_type=jnp.float32
    ).astype(jnp.bfloat16)
    back = lax.all_to_all(expert_out, "ctx", split_axis=0, concat_axis=0, tiled=True)
    combine_map = (
        (one_hot * expert_weights.reshape(-1)[:, None]).reshape(rows_dev, TOP, n_slots).sum(1)
    )
    expert_sum = jnp.dot(
        combine_map,
        back.reshape(n_slots, normed.shape[1]).astype(jnp.float32),
        precision=lax.Precision.HIGHEST,
    )
    return (state + expert_sum).astype(jnp.bfloat16)


LANES = 128
SUB = 8
MESH = pl.DeviceIdType.MESH
F32 = jnp.float32
BF16 = jnp.bfloat16
Q, K, V, NEW, NUM, STAT, PROJ, ROWS, BACK, PROJ_PAIR, ROWS_PAIR, BACK_PAIR = range(12)
KINDS = 12


def shuffled(team, i):
    return (i % 2) * (team // 2) + i // 2


def fits(shards, rows_dev, width, capacity, experts_dev):
    team = shards // KV_HEADS
    if shards % KV_HEADS or team == 0 or (HEADS // KV_HEADS) % team:
        return False
    pair = HEADS // KV_HEADS // team
    return (
        experts_dev == 1
        and team == KV_HEADS
        and team % 2 == 0
        and all(shuffled(team, shuffled(team, i)) == i for i in range(team))
        and HEAD_DIM == LANES
        and shards * SUB == LANES
        and (shards * rows_dev) % (2 * SUB) == 0
        and pair * rows_dev <= SUB - 2
        and rows_dev <= team
        and shards <= LANES
        and capacity >= rows_dev
        and width % (2 * SUB * LANES) == 0
    )


def layer_kernel(
    shards,
    q_hbm,
    ck_ref,
    cv_ref,
    nk_hbm,
    nv_hbm,
    len_ref,
    res_hbm,
    wo_ref,
    gain_hbm,
    wg_ref,
    wu_ref,
    wd_ref,
    ids_hbm,
    ew_hbm,
    out_ref,
    wo,
    wg,
    wu,
    wd,
    q_wide,
    q_send,
    q_recv,
    q_heads,
    k_all,
    v_all,
    new_wide,
    new_send,
    new_recv,
    num_send,
    num_recv,
    stat_send,
    stat_recv,
    stage,
    proj_send,
    proj_recv,
    res_wide,
    gain_wide,
    mix_all,
    mix,
    row_send,
    row_recv,
    x_all,
    act,
    back_away,
    back_near,
    back_send,
    back_recv,
    q_ref,
    nk_ref,
    nv_ref,
    res_ref,
    gain_ref,
    ids_ref,
    ew_ref,
    load_sem,
    send_sem,
    recv_sem,
):
    me = lax.axis_index("ctx")
    team = shards // KV_HEADS
    pair = HEADS // KV_HEADS // team
    rows_dev, width = res_hbm.shape
    chunks = width // LANES
    cache = ck_ref.shape[0]
    plane, mate = me // team, me % team
    swap = functools.partial(shuffled, team)
    head = swap(mate)
    chips = shards // 2
    chip, core = me // 2, me % 2
    sibling = me + 1 - 2 * core

    barrier = pltpu.get_barrier_semaphore()

    def greet(step, carry):
        pl.semaphore_signal(
            barrier, inc=1, device_id={"ctx": lax.rem(me + step, shards)}, device_id_type=MESH
        )
        return carry

    lax.fori_loop(1, shards, greet, 0)

    own_lanes = pl.ds(pl.multiple_of(head * LANES, LANES), LANES)
    small = [
        (q_hbm, q_ref),
        (nk_hbm, nk_ref),
        (nv_hbm, nv_ref),
        (res_hbm, res_ref),
        (gain_hbm, gain_ref),
        (ids_hbm, ids_ref),
        (ew_hbm, ew_ref),
    ]
    large = [
        (ck_ref.at[:, own_lanes], k_all.at[mate]),
        (cv_ref.at[:, own_lanes], v_all.at[mate]),
        (wo_ref, wo.at[core]),
        (wg_ref.at[0], wg),
        (wu_ref.at[0], wu),
        (wd_ref.at[0], wd),
    ]
    loads = [
        pltpu.make_async_copy(src, dst, load_sem.at[i])
        for i, (src, dst) in enumerate(small + large)
    ]
    for load in loads:
        load.start()
    for load in loads[: len(small)]:
        load.wait()
    loads = loads[len(small) :]

    q_wide[...] = jnp.zeros_like(q_wide)
    for one in range(HEADS):
        kv, rest = divmod(one, HEADS // KV_HEADS)
        who, which = divmod(rest, pair)
        q_wide[kv, pl.ds(who * SUB + which * rows_dev, rows_dev), :] = q_ref[
            :, one * LANES : (one + 1) * LANES
        ].astype(F32)
    expert = lax.broadcasted_iota(jnp.int32, (rows_dev, LANES), 1)
    routed = jnp.zeros((rows_dev, LANES), F32)
    for k in range(TOP):
        routed += jnp.where(expert == ids_ref[:, k : k + 1], ew_ref[:, k : k + 1], 0.0)
    coarse = routed.astype(BF16).astype(F32)
    fine = routed - coarse
    for kv in range(KV_HEADS):
        for r in range(rows_dev):
            q_wide[kv, (r + 1) * SUB - 2 : (r + 1) * SUB - 1, :] = coarse[r : r + 1]
            q_wide[kv, (r + 1) * SUB - 1 : (r + 1) * SUB, :] = fine[r : r + 1]
    q_send[...] = q_wide[...].astype(BF16)
    new_wide[...] = jnp.zeros_like(new_wide)
    live = jnp.full((1, LANES), len_ref[0], jnp.int32).astype(F32)
    for kv in range(KV_HEADS):
        lanes = slice(kv * LANES, (kv + 1) * LANES)
        new_wide[kv, 0:rows_dev, :] = nk_ref[:, lanes].astype(F32)
        new_wide[kv, rows_dev : rows_dev + 1, :] = live
        new_wide[kv, SUB : SUB + rows_dev, :] = nv_ref[:, lanes].astype(F32)
    new_send[...] = new_wide[...].astype(BF16)

    def remote(kind, src, dst, target, source):
        return pltpu.make_async_remote_copy(
            src_ref=src,
            dst_ref=dst,
            send_sem=send_sem.at[kind, target],
            recv_sem=recv_sem.at[kind, source],
            device_id={"ctx": target},
            device_id_type=MESH,
        )

    def near(step):
        other = lax.rem(mate + step, team)
        return other, plane * team + other

    def key_copies(target_mate, target, source_mate):
        lane_head = swap(target_mate)
        lanes = pl.ds(pl.multiple_of(lane_head * LANES, LANES), LANES)
        source = plane * team + source_mate
        return (
            remote(K, ck_ref.at[:, lanes], k_all.at[source_mate], target, source),
            remote(V, cv_ref.at[:, lanes], v_all.at[source_mate], target, source),
            remote(NEW, new_send.at[lane_head], new_recv.at[source_mate], target, source),
        )

    pl.semaphore_wait(barrier, shards - 1)

    def peers(body):
        def step_body(step, carry):
            body(lax.rem(me + step, shards))
            return carry

        lax.fori_loop(1, shards, step_body, 0)

    def q_copy(target, source):
        return remote(Q, q_send.at[swap(target % team)], q_recv.at[source], target, source)

    peers(lambda other: q_copy(other, me).start())
    for step in range(1, team):
        for copy in key_copies(*near(step), mate):
            copy.start()

    def weight_copy(target, source, source_core):
        return remote(PROJ_PAIR, wo_ref, wo.at[source_core], target, source)

    weight_copy(sibling, me, core).start()

    q_recv[me] = q_send[head]
    new_recv[mate] = new_send[head]

    for c in range(chunks):
        lanes = slice(c * LANES, (c + 1) * LANES)
        res_wide[pl.ds(c, rows_dev, stride=chunks), :] = res_ref[:, lanes].astype(F32)
        gain_wide[c : c + 1, :] = gain_ref[lanes].astype(F32).reshape(1, LANES)

    peers(lambda other: q_copy(me, other).wait_recv())
    gathered = q_recv[...].astype(F32).reshape(shards, team, SUB, LANES)
    split = gathered.reshape(chips, 2, team, SUB, LANES)
    for one in range(team):
        first = one // 2 * 2
        q_heads[one] = (
            split[:, one % 2, first : first + 2].reshape(shards * SUB, LANES).astype(BF16)
        )
    at_lane = lax.broadcasted_iota(jnp.int32, (shards, LANES), 1)
    for r in range(rows_dev):
        both = gathered[:, r, SUB - 2, :] + gathered[:, r, SUB - 1, :]
        mine = jnp.sum(jnp.where(at_lane == me, both, 0.0), axis=1, keepdims=True)
        mix_all[...] = jnp.broadcast_to(mine, (shards, LANES))
        for half in range(2):
            mix[pl.ds(half * chips * rows_dev + r, chips, stride=rows_dev), :] = mix_all[
                pl.ds(half, chips, stride=2), :
            ]
    loads[0].wait()
    loads[1].wait()
    for step in range(1, team):
        other, _ = near(step)
        for copy in key_copies(mate, me, other):
            copy.wait_recv()

    n_cache = team * cache
    n_new = team * SUB
    fresh = new_recv[...].astype(F32)
    new_k = fresh[:, 0:SUB].reshape(n_new, LANES).astype(BF16)
    new_v = fresh[:, SUB : 2 * SUB].reshape(n_new, LANES).astype(BF16)
    lengths = fresh[:, rows_dev : rows_dev + 1, :]
    spot = lax.broadcasted_iota(jnp.int32, (team, cache, LANES), 1).astype(F32)
    cache_ok = (spot < lengths).reshape(n_cache, LANES)
    lane = lax.broadcasted_iota(jnp.int32, (n_new, LANES), 1)
    place = lax.broadcasted_iota(jnp.int32, (n_new, LANES), 0)
    key_at = place % SUB
    span = (plane * team + place // SUB) * rows_dev + key_at
    across = (((1,), (1,)), ((), ()))
    down = (((0,), (0,)), ((), ()))
    scale = HEAD_DIM ** (-0.5)
    stat_row = lax.broadcasted_iota(jnp.int32, (SUB, LANES), 0)

    def head_copies(target, target_mate, source, source_plane):
        return (
            remote(NUM, num_send.at[target_mate], num_recv.at[source_plane], target, source),
            remote(STAT, stat_send.at[target_mate], stat_recv.at[source_plane], target, source),
        )

    def attend(step, carry):
        to = lax.rem(plane + step, team)
        queries = q_heads[to]
        owner = lane // (2 * SUB) * 2 + to % 2
        new_ok = (key_at < rows_dev) & (span <= owner * rows_dev + (lane % SUB) % rows_dev)
        keys = k_all[...].reshape(n_cache, LANES)
        old = lax.dot_general(keys, queries, across, preferred_element_type=F32) * scale
        new = lax.dot_general(new_k, queries, across, preferred_element_type=F32) * scale
        old = jnp.where(cache_ok, old, MASKED)
        new = jnp.where(new_ok, new, MASKED)
        top = jnp.maximum(
            jnp.max(old, axis=0, keepdims=True), jnp.max(new, axis=0, keepdims=True)
        )
        old = jnp.where(cache_ok, jnp.exp(old - top), 0.0)
        new = jnp.where(new_ok, jnp.exp(new - top), 0.0)
        total = jnp.sum(old, axis=0, keepdims=True) + jnp.sum(new, axis=0, keepdims=True)
        values = v_all[...].reshape(n_cache, LANES)
        numer = lax.dot_general(values, old.astype(BF16), down, preferred_element_type=F32)
        numer += lax.dot_general(new_v, new.astype(BF16), down, preferred_element_type=F32)
        num_send[to] = numer.astype(BF16)
        stat_send[to] = jnp.where(stat_row == 0, top, total)

        target = head * team + to

        @pl.when(target != me)
        def _():
            for copy in head_copies(target, to, me, plane):
                copy.start()

        @pl.when(target == me)
        def _():
            num_recv[plane] = num_send[to]
            stat_recv[plane] = stat_send[to]

        return carry

    lax.fori_loop(0, team, attend, 0)
    for at in range(team):
        source = at * team + swap(plane)

        @pl.when(source != me)
        def _():
            for copy in head_copies(me, mate, source, at):
                copy.wait_recv()

    tops = stat_recv[:, 0:1, :]
    weight = jnp.exp(tops - jnp.max(tops, axis=0, keepdims=True))
    weight = weight / jnp.sum(weight * stat_recv[:, 1:2, :], axis=0, keepdims=True)
    attention = jnp.sum(num_recv[...].astype(F32) * weight, axis=0).astype(BF16)

    n_rows = shards * rows_dev
    tile_row = lax.broadcasted_iota(jnp.int32, (n_rows // 2, LANES), 0)
    tile_lane = lax.broadcasted_iota(jnp.int32, (n_rows // 2, LANES), 1)
    parts = []
    for which in range(2 * pair):
        place = which // pair * SUB + which % pair * rows_dev
        pick = (tile_row // rows_dev == tile_lane // (2 * SUB)) & (
            tile_lane % (2 * SUB) == place + tile_row % rows_dev
        )
        pick = jnp.where(pick, 1.0, 0.0).astype(BF16)
        parts.append(
            lax.dot_general(pick, attention, across, preferred_element_type=F32).astype(BF16)
        )
    columns = jnp.concatenate(parts, axis=1)

    def spread(first, tile):
        for j in range(tile.shape[1] // LANES):
            stage[pl.ds(first + j, tile.shape[0], stride=chunks), :] = tile[
                :, j * LANES : (j + 1) * LANES
            ]

    loads[2].wait()
    weight_copy(me, sibling, 1 - core).wait_recv()
    wide = 4 * LANES
    for at in range(width // wide):
        part = wo[:, :, at * wide : (at + 1) * wide].reshape(columns.shape[1], wide)
        tile = jnp.dot(columns, part, preferred_element_type=F32)
        spread(4 * at, tile)

    half_rows = chips * rows_dev * chunks
    own_half = pl.ds(pl.multiple_of(core * half_rows, half_rows), half_rows)
    away_half = pl.ds(pl.multiple_of((1 - core) * half_rows, half_rows), half_rows)

    def others(body):
        def step_body(step, carry):
            body(lax.rem(chip + step, chips))
            return carry

        lax.fori_loop(1, chips, step_body, 0)

    def chip_copy(kind, send, recv, target_chip, source_chip):
        return remote(
            kind,
            send.at[target_chip],
            recv.at[source_chip],
            target_chip * 2 + core,
            source_chip * 2 + core,
        )

    def proj_copy(target_chip, source_chip):
        return chip_copy(PROJ, proj_send, proj_recv, target_chip, source_chip)

    def back_copy(target_chip, source_chip):
        return chip_copy(BACK, back_send, back_recv, target_chip, source_chip)

    def back_pair_copy(target, source):
        return remote(BACK_PAIR, back_away, back_near, target, source)

    proj_send[...] = stage[0:half_rows, :].astype(BF16).reshape(proj_send.shape)
    others(lambda other: proj_copy(other, chip).start())
    proj_recv[chip] = proj_send[chip]
    others(lambda other: proj_copy(chip, other).wait_recv())
    state = res_wide[...] + jnp.sum(proj_recv[...].astype(F32), axis=0)
    state = state.reshape(rows_dev, chunks, LANES)
    squares = jnp.sum(jnp.sum(state * state, axis=1, keepdims=True), axis=2, keepdims=True)
    normed = state * lax.rsqrt(squares / width + epsilon) * gain_wide[...][None]
    normed = normed.reshape(rows_dev * chunks, LANES)
    row_send[...] = normed.astype(BF16)

    def row_copy(target, source_chip):
        source = source_chip * 2 + core
        return remote(ROWS, row_send, row_recv.at[core * chips + source_chip], target, source)

    def row_pair_copy(target, source, at):
        block = row_recv.at[at]
        return pltpu.make_async_remote_copy(
            src_ref=block,
            dst_ref=block,
            send_sem=send_sem.at[ROWS_PAIR, at],
            recv_sem=recv_sem.at[ROWS_PAIR, at],
            device_id={"ctx": target},
            device_id_type=MESH,
        )

    others(lambda other: row_copy(other * 2 + core, chip).start())
    row_recv[core * chips + chip] = row_send[...]
    row_pair_copy(sibling, me, core * chips + chip).start()

    def hand_on(other):
        row_copy(me, other).wait_recv()
        row_pair_copy(sibling, me, core * chips + other).start()

    others(hand_on)

    def handed(at, carry):
        row_pair_copy(me, sibling, (1 - core) * chips + at).wait_recv()
        return carry

    lax.fori_loop(0, chips, handed, 0)
    stage[...] = row_recv[...].astype(F32).reshape(stage.shape)
    for c in range(chunks):
        x_all[:, c * LANES : (c + 1) * LANES] = stage[
            pl.ds(c, n_rows, stride=chunks), :
        ].astype(BF16)

    loads[3].wait()
    loads[4].wait()
    hidden = act.shape[1]
    step_cols = 2 * LANES if hidden % (2 * LANES) == 0 else LANES
    for at in range(hidden // step_cols):
        lanes = slice(at * step_cols, (at + 1) * step_cols)
        gate = jnp.dot(x_all[...], wg[:, lanes], preferred_element_type=F32)
        up = jnp.dot(x_all[...], wu[:, lanes], preferred_element_type=F32)
        act[:, lanes] = (gate / (1.0 + jnp.exp(-gate)) * up).astype(BF16)
    loads[5].wait()
    for at in range(width // wide):
        tile = jnp.dot(act[...], wd[:, at * wide : (at + 1) * wide], preferred_element_type=F32)
        spread(4 * at, tile * jnp.concatenate([mix[...]] * 4, axis=1))
    back_away[...] = stage[away_half, :].astype(BF16).reshape(back_away.shape)
    back_pair_copy(sibling, me).start()
    back_pair_copy(me, sibling).wait_recv()
    summed = stage[own_half, :].reshape(back_near.shape) + back_near[...].astype(F32)
    back_send[...] = summed.astype(BF16)
    others(lambda other: back_copy(other, chip).start())
    back_recv[chip] = back_send[chip]

    for step in range(1, team):
        for copy in key_copies(*near(step), mate):
            copy.wait_send()
    for at in range(team):
        target = head * team + at

        @pl.when(target != me)
        def _():
            for copy in head_copies(target, at, me, plane):
                copy.wait_send()

    peers(lambda other: q_copy(other, me).wait_send())
    weight_copy(sibling, me, core).wait_send()
    back_pair_copy(sibling, me).wait_send()

    def sent(other):
        proj_copy(other, chip).wait_send()
        row_copy(other * 2 + core, chip).wait_send()
        row_pair_copy(sibling, me, core * chips + other).wait_send()

    others(sent)
    row_pair_copy(sibling, me, core * chips + chip).wait_send()
    others(lambda other: back_copy(chip, other).wait_recv())
    final = state + jnp.sum(back_recv[...].astype(F32), axis=0).reshape(state.shape)
    for r in range(rows_dev):
        res_wide[r * chunks : (r + 1) * chunks, :] = final[r]
    for c in range(chunks):
        out_ref[:, c * LANES : (c + 1) * LANES] = res_wide[
            pl.ds(c, rows_dev, stride=chunks), :
        ].astype(BF16)
    others(lambda other: back_copy(other, chip).wait_send())


def local(*args):
    (queries, cache_keys, _, _, _, _, residual_in, out_weight, _, expert_gate) = args[:10]
    shards = lax.axis_size("ctx")
    rows_dev, width = residual_in.shape
    capacity = max(2, 2 * rows_dev * TOP // shards)
    if not fits(shards, rows_dev, width, capacity, expert_gate.shape[0]):
        return plain(*args)
    team = shards // KV_HEADS
    hidden = expert_gate.shape[2]
    cache = cache_keys.shape[0]
    rows = rows_dev * width // LANES
    any_spec = pl.BlockSpec(memory_space=pl.ANY)
    vmem = pl.BlockSpec(memory_space=pltpu.VMEM)
    smem = pl.BlockSpec(memory_space=pltpu.SMEM)
    blocks = pltpu.VMEM((shards, rows, LANES), BF16)
    halves = pltpu.VMEM((shards // 2, rows, LANES), BF16)
    tiles = pltpu.VMEM((team, LANES, shards * SUB), BF16)
    stats = pltpu.VMEM((team, SUB, LANES), F32)
    keys = pltpu.VMEM((team, cache, LANES), BF16)
    new = pltpu.VMEM((KV_HEADS, 2 * SUB, LANES), BF16)
    flops = 2 * shards * rows_dev * width * (3 * hidden + out_weight.shape[0])
    return pl.pallas_call(
        functools.partial(layer_kernel, shards),
        out_shape=jax.ShapeDtypeStruct((rows_dev, width), BF16),
        in_specs=[any_spec] * 5 + [smem] + [any_spec] * 8,
        out_specs=vmem,
        scratch_shapes=[
            pltpu.VMEM((2, *out_weight.shape), BF16),
            pltpu.VMEM((width, hidden), BF16),
            pltpu.VMEM((width, hidden), BF16),
            pltpu.VMEM((hidden, width), BF16),
            pltpu.VMEM((KV_HEADS, team * SUB, LANES), F32),
            pltpu.VMEM((KV_HEADS, team * SUB, LANES), BF16),
            pltpu.VMEM((shards, team * SUB, LANES), BF16),
            pltpu.VMEM((team, shards * SUB, LANES), BF16),
            keys,
            keys,
            pltpu.VMEM((KV_HEADS, 2 * SUB, LANES), F32),
            new,
            new,
            tiles,
            tiles,
            stats,
            stats,
            pltpu.VMEM((shards * rows, LANES), F32),
            halves,
            halves,
            pltpu.VMEM((rows, LANES), F32),
            pltpu.VMEM((width // LANES, LANES), F32),
            pltpu.VMEM((shards, LANES), F32),
            pltpu.VMEM((shards * rows_dev, LANES), F32),
            pltpu.VMEM((rows, LANES), BF16),
            blocks,
            pltpu.VMEM((shards * rows_dev, width), BF16),
            pltpu.VMEM((shards * rows_dev, hidden), BF16),
            halves,
            halves,
            halves,
            halves,
            *(pltpu.VMEM(args[i].shape, args[i].dtype) for i in (0, 3, 4, 6)),
            pltpu.VMEM((width,), BF16),
            *(pltpu.VMEM(args[i].shape, args[i].dtype) for i in (12, 13)),
            pltpu.SemaphoreType.DMA((13,)),
            pltpu.SemaphoreType.DMA((KINDS, shards)),
            pltpu.SemaphoreType.DMA((KINDS, shards)),
        ],
        compiler_params=pltpu.CompilerParams(
            collective_id=0, has_side_effects=True, vmem_limit_bytes=60 * 1024 * 1024
        ),
        cost_estimate=pl.CostEstimate(
            flops=flops, bytes_accessed=2 * 3 * hidden * width, transcendentals=0
        ),
    )(*args)


def solution(mesh):
    placed = (
        P(("groups", "ctx"), None),
        P(("groups", "ctx"), None),
        P(("groups", "ctx"), None),
        P(("groups", "ctx"), None),
        P(("groups", "ctx"), None),
        P(("groups", "ctx")),
        P(("groups", "ctx"), None),
        P("ctx", None),
        P(),
        P("ctx", None, None),
        P("ctx", None, None),
        P("ctx", None, None),
        P(("groups", "ctx"), None),
        P(("groups", "ctx"), None),
    )
    return jax.shard_map(
        local, mesh=mesh, in_specs=placed, out_specs=P(("groups", "ctx"), None), check_vma=False
    )
```

```python
import functools

import jax
import jax.numpy as jnp
from jax import lax
from jax.experimental import pallas as pl
from jax.experimental.pallas import tpu as pltpu
from jax.sharding import PartitionSpec as P

HEADS = 32
KV_HEADS = 4
HEAD_DIM = 128
TOP = 8


MASKED = -1e30
epsilon = 1e-06


def plain(
    queries,
    cache_keys,
    cache_values,
    new_keys,
    new_values,
    cache_lengths,
    residual_in,
    out_weight,
    norm_gain,
    expert_gate,
    expert_up,
    expert_down,
    expert_ids,
    expert_weights,
):
    shards = lax.axis_size("ctx")
    device = lax.axis_index("ctx")
    rows_dev = residual_in.shape[0]
    capacity = max(2, 2 * rows_dev * TOP // shards)
    group_size = HEADS // KV_HEADS
    whole_queries = lax.all_gather(queries, "ctx", axis=0, tiled=True)
    all_rows = whole_queries.shape[0]
    query_heads = whole_queries.reshape(all_rows, KV_HEADS, group_size, HEAD_DIM)
    local_cache = cache_keys.shape[0]
    key_rows = jnp.concatenate([cache_keys, new_keys], 0).reshape(
        local_cache + rows_dev, KV_HEADS, HEAD_DIM
    )
    value_rows = jnp.concatenate([cache_values, new_values], 0).reshape(
        local_cache + rows_dev, KV_HEADS, HEAD_DIM
    )
    slot_ids = jnp.arange(local_cache + rows_dev, dtype=jnp.int32)
    span_pos = device * rows_dev + slot_ids - local_cache
    row_ids = jnp.arange(all_rows, dtype=jnp.int32)
    usable = jnp.where(
        slot_ids[None, :] < local_cache,
        (slot_ids < cache_lengths[0])[None, :],
        span_pos[None, :] <= row_ids[:, None],
    )
    scores = jnp.einsum(
        "rkgd,nkd->kgrn", query_heads, key_rows, preferred_element_type=jnp.float32
    ) * HEAD_DIM ** (-0.5)
    scores = jnp.where(usable, scores, MASKED)
    maxima = jnp.max(scores, axis=-1)
    exp_weights = jnp.where(usable, jnp.exp(scores - maxima[..., None]), 0.0)
    totals = jnp.sum(exp_weights, axis=-1)
    numerators = jnp.einsum(
        "kgrn,nkd->rkgd",
        exp_weights.astype(jnp.bfloat16),
        value_rows,
        preferred_element_type=jnp.float32,
    ).reshape(all_rows, HEADS, HEAD_DIM)
    maxima = maxima.transpose(2, 0, 1).reshape(all_rows, HEADS)
    totals = totals.transpose(2, 0, 1).reshape(all_rows, HEADS)
    largest = lax.pmax(maxima, "ctx")
    rescale = jnp.exp(maxima - largest)
    denoms = lax.psum(totals * rescale, "ctx")
    weighted = (numerators * (rescale / denoms)[..., None]).reshape(all_rows, HEADS * HEAD_DIM)
    columns = lax.psum_scatter(weighted, "ctx", scatter_dimension=1, tiled=True).astype(
        jnp.bfloat16
    )
    projected = lax.psum_scatter(
        jnp.dot(columns, out_weight, preferred_element_type=jnp.float32),
        "ctx",
        scatter_dimension=0,
        tiled=True,
    )
    state = residual_in.astype(jnp.float32) + projected
    normed = (
        state
        * lax.rsqrt(jnp.mean(state * state, axis=1, keepdims=True) + epsilon)
        * norm_gain.astype(jnp.float32)
    ).astype(jnp.bfloat16)
    n_slots = shards * capacity
    flat_ids = expert_ids.reshape(-1)
    places = jnp.arange(flat_ids.shape[0], dtype=jnp.int32)
    earlier = (flat_ids[:, None] == flat_ids[None, :]) & (places[None, :] < places[:, None])
    slot_of = flat_ids * capacity + jnp.sum(earlier.astype(jnp.int32), axis=1)
    one_hot = (slot_of[:, None] == jnp.arange(n_slots, dtype=jnp.int32)[None, :]).astype(
        jnp.float32
    )
    dispatch_map = one_hot.reshape(rows_dev, TOP, n_slots).sum(1)
    outgoing = (
        jnp.dot(dispatch_map.T.astype(jnp.bfloat16), normed, preferred_element_type=jnp.float32)
        .astype(jnp.bfloat16)
        .reshape(shards, capacity, normed.shape[1])
    )
    received = lax.all_to_all(outgoing, "ctx", split_axis=0, concat_axis=0, tiled=True)
    gate_out = jnp.einsum(
        "scd,df->scf", received, expert_gate[0], preferred_element_type=jnp.float32
    )
    up_out = jnp.einsum("scd,df->scf", received, expert_up[0], preferred_element_type=jnp.float32)
    activated = (jax.nn.silu(gate_out) * up_out).astype(jnp.bfloat16)
    expert_out = jnp.einsum(
        "scf,fd->scd", activated, expert_down[0], preferred_element_type=jnp.float32
    ).astype(jnp.bfloat16)
    back = lax.all_to_all(expert_out, "ctx", split_axis=0, concat_axis=0, tiled=True)
    combine_map = (
        (one_hot * expert_weights.reshape(-1)[:, None]).reshape(rows_dev, TOP, n_slots).sum(1)
    )
    expert_sum = jnp.dot(
        combine_map,
        back.reshape(n_slots, normed.shape[1]).astype(jnp.float32),
        precision=lax.Precision.HIGHEST,
    )
    return (state + expert_sum).astype(jnp.bfloat16)


LANES = 128
SUB = 8
MESH = pl.DeviceIdType.MESH
F32 = jnp.float32
BF16 = jnp.bfloat16
Q, K, V, NEW, NUM, STAT, PROJ, ROWS, BACK, PROJ_PAIR, ROWS_PAIR, BACK_PAIR = range(12)
KINDS = 12


def shuffled(team, i):
    return (i % 2) * (team // 2) + i // 2


def fits(shards, rows_dev, width, capacity, experts_dev):
    team = shards // KV_HEADS
    if shards % KV_HEADS or team == 0 or (HEADS // KV_HEADS) % team:
        return False
    pair = HEADS // KV_HEADS // team
    return (
        experts_dev == 1
        and team == KV_HEADS
        and team % 2 == 0
        and all(shuffled(team, shuffled(team, i)) == i for i in range(team))
        and HEAD_DIM == LANES
        and shards * SUB == LANES
        and (shards * rows_dev) % (2 * SUB) == 0
        and pair * rows_dev <= SUB - 2
        and rows_dev <= team
        and shards <= LANES
        and capacity >= rows_dev
        and width % (2 * SUB * LANES) == 0
    )


def layer_kernel(
    shards,
    q_hbm,
    ck_ref,
    cv_ref,
    nk_hbm,
    nv_hbm,
    len_ref,
    res_hbm,
    wo_ref,
    gain_hbm,
    wg_ref,
    wu_ref,
    wd_ref,
    ids_hbm,
    ew_hbm,
    out_ref,
    wo,
    wg,
    wu,
    wd,
    q_wide,
    q_send,
    q_recv,
    q_heads,
    k_all,
    v_all,
    values_t,
    new_wide,
    new_send,
    new_recv,
    num_send,
    num_recv,
    stat_send,
    stat_recv,
    stage,
    proj_send,
    proj_recv,
    res_wide,
    gain_wide,
    mix_all,
    mix,
    row_send,
    row_recv,
    x_all,
    act,
    back_away,
    back_near,
    back_send,
    back_recv,
    q_ref,
    nk_ref,
    nv_ref,
    res_ref,
    gain_ref,
    ids_ref,
    ew_ref,
    load_sem,
    send_sem,
    recv_sem,
):
    me = lax.axis_index("ctx")
    team = shards // KV_HEADS
    pair = HEADS // KV_HEADS // team
    rows_dev, width = res_hbm.shape
    chunks = width // LANES
    cache = ck_ref.shape[0]
    plane, mate = me // team, me % team
    swap = functools.partial(shuffled, team)
    head = swap(mate)
    chips = shards // 2
    chip, core = me // 2, me % 2
    sibling = me + 1 - 2 * core

    barrier = pltpu.get_barrier_semaphore()

    def greet(step, carry):
        pl.semaphore_signal(
            barrier, inc=1, device_id={"ctx": lax.rem(me + step, shards)}, device_id_type=MESH
        )
        return carry

    lax.fori_loop(1, shards, greet, 0)

    own_lanes = pl.ds(pl.multiple_of(head * LANES, LANES), LANES)
    small = [
        (q_hbm, q_ref),
        (nk_hbm, nk_ref),
        (nv_hbm, nv_ref),
        (res_hbm, res_ref),
        (gain_hbm, gain_ref),
        (ids_hbm, ids_ref),
        (ew_hbm, ew_ref),
    ]
    large = [
        (ck_ref.at[:, own_lanes], k_all.at[mate]),
        (cv_ref.at[:, own_lanes], v_all.at[mate]),
        (wo_ref, wo.at[core]),
        (wg_ref.at[0], wg),
        (wu_ref.at[0], wu),
        (wd_ref.at[0], wd),
    ]
    loads = [
        pltpu.make_async_copy(src, dst, load_sem.at[i])
        for i, (src, dst) in enumerate(small + large)
    ]
    for load in loads:
        load.start()
    for load in loads[: len(small)]:
        load.wait()
    loads = loads[len(small) :]

    q_wide[...] = jnp.zeros_like(q_wide)
    for one in range(HEADS):
        kv, rest = divmod(one, HEADS // KV_HEADS)
        who, which = divmod(rest, pair)
        q_wide[kv, pl.ds(who * SUB + which * rows_dev, rows_dev), :] = q_ref[
            :, one * LANES : (one + 1) * LANES
        ].astype(F32)
    expert = lax.broadcasted_iota(jnp.int32, (rows_dev, LANES), 1)
    routed = jnp.zeros((rows_dev, LANES), F32)
    for k in range(TOP):
        routed += jnp.where(expert == ids_ref[:, k : k + 1], ew_ref[:, k : k + 1], 0.0)
    coarse = routed.astype(BF16).astype(F32)
    fine = routed - coarse
    for kv in range(KV_HEADS):
        for r in range(rows_dev):
            q_wide[kv, (r + 1) * SUB - 2 : (r + 1) * SUB - 1, :] = coarse[r : r + 1]
            q_wide[kv, (r + 1) * SUB - 1 : (r + 1) * SUB, :] = fine[r : r + 1]
    q_send[...] = q_wide[...].astype(BF16)
    new_wide[...] = jnp.zeros_like(new_wide)
    live = jnp.full((1, LANES), len_ref[0], jnp.int32).astype(F32)
    for kv in range(KV_HEADS):
        lanes = slice(kv * LANES, (kv + 1) * LANES)
        new_wide[kv, 0:rows_dev, :] = nk_ref[:, lanes].astype(F32)
        new_wide[kv, rows_dev : rows_dev + 1, :] = live
        new_wide[kv, SUB : SUB + rows_dev, :] = nv_ref[:, lanes].astype(F32)
    new_send[...] = new_wide[...].astype(BF16)

    def remote(kind, src, dst, target, source):
        return pltpu.make_async_remote_copy(
            src_ref=src,
            dst_ref=dst,
            send_sem=send_sem.at[kind, target],
            recv_sem=recv_sem.at[kind, source],
            device_id={"ctx": target},
            device_id_type=MESH,
        )

    def near(step):
        other = lax.rem(mate + step, team)
        return other, plane * team + other

    def key_copies(target_mate, target, source_mate):
        lane_head = swap(target_mate)
        lanes = pl.ds(pl.multiple_of(lane_head * LANES, LANES), LANES)
        source = plane * team + source_mate
        return (
            remote(K, ck_ref.at[:, lanes], k_all.at[source_mate], target, source),
            remote(V, cv_ref.at[:, lanes], v_all.at[source_mate], target, source),
            remote(NEW, new_send.at[lane_head], new_recv.at[source_mate], target, source),
        )

    pl.semaphore_wait(barrier, shards - 1)

    def peers(body):
        def step_body(step, carry):
            body(lax.rem(me + step, shards))
            return carry

        lax.fori_loop(1, shards, step_body, 0)

    def q_copy(target, source):
        return remote(Q, q_send.at[swap(target % team)], q_recv.at[source], target, source)

    peers(lambda other: q_copy(other, me).start())
    for step in range(1, team):
        for copy in key_copies(*near(step), mate):
            copy.start()

    def weight_copy(target, source, source_core):
        return remote(PROJ_PAIR, wo_ref, wo.at[source_core], target, source)

    weight_copy(sibling, me, core).start()

    q_recv[me] = q_send[head]
    new_recv[mate] = new_send[head]

    for c in range(chunks):
        lanes = slice(c * LANES, (c + 1) * LANES)
        res_wide[pl.ds(c, rows_dev, stride=chunks), :] = res_ref[:, lanes].astype(F32)
        gain_wide[c : c + 1, :] = gain_ref[lanes].astype(F32).reshape(1, LANES)

    peers(lambda other: q_copy(me, other).wait_recv())
    gathered = q_recv[...].astype(F32).reshape(shards, team, SUB, LANES)
    split = gathered.reshape(chips, 2, team, SUB, LANES)
    for one in range(team):
        first = one // 2 * 2
        q_heads[one] = (
            split[:, one % 2, first : first + 2].reshape(shards * SUB, LANES).astype(BF16)
        )
    at_lane = lax.broadcasted_iota(jnp.int32, (shards, LANES), 1)
    for r in range(rows_dev):
        both = gathered[:, r, SUB - 2, :] + gathered[:, r, SUB - 1, :]
        mine = jnp.sum(jnp.where(at_lane == me, both, 0.0), axis=1, keepdims=True)
        mix_all[...] = jnp.broadcast_to(mine, (shards, LANES))
        for half in range(2):
            mix[pl.ds(half * chips * rows_dev + r, chips, stride=rows_dev), :] = mix_all[
                pl.ds(half, chips, stride=2), :
            ]
    loads[0].wait()
    loads[1].wait()
    for step in range(1, team):
        other, _ = near(step)
        for copy in key_copies(mate, me, other):
            copy.wait_recv()

    n_cache = team * cache
    n_new = team * SUB
    fresh = new_recv[...].astype(F32)
    new_k = fresh[:, 0:SUB].reshape(n_new, LANES).astype(BF16)
    new_v = fresh[:, SUB : 2 * SUB].reshape(n_new, LANES).astype(BF16)
    lengths = fresh[:, rows_dev : rows_dev + 1, :]
    spot = lax.broadcasted_iota(jnp.int32, (team, cache, LANES), 1).astype(F32)
    cache_ok = (spot < lengths).reshape(n_cache, LANES)
    lane = lax.broadcasted_iota(jnp.int32, (n_new, LANES), 1)
    place = lax.broadcasted_iota(jnp.int32, (n_new, LANES), 0)
    key_at = place % SUB
    span = (plane * team + place // SUB) * rows_dev + key_at
    across = (((1,), (1,)), ((), ()))
    down = (((0,), (0,)), ((), ()))
    scale = HEAD_DIM ** (-0.5)
    stat_row = lax.broadcasted_iota(jnp.int32, (SUB, LANES), 0)

    values_t[...] = v_all[...].reshape(n_cache, LANES).T

    def head_copies(target, target_mate, source, source_plane):
        return (
            remote(NUM, num_send.at[target_mate], num_recv.at[source_plane], target, source),
            remote(STAT, stat_send.at[target_mate], stat_recv.at[source_plane], target, source),
        )

    def attend(step, carry):
        to = lax.rem(plane + step, team)
        queries = q_heads[to]
        owner = lane // (2 * SUB) * 2 + to % 2
        new_ok = (key_at < rows_dev) & (span <= owner * rows_dev + (lane % SUB) % rows_dev)
        keys = k_all[...].reshape(n_cache, LANES)
        old = lax.dot_general(keys, queries, across, preferred_element_type=F32) * scale
        new = lax.dot_general(new_k, queries, across, preferred_element_type=F32) * scale
        old = jnp.where(cache_ok, old, MASKED)
        new = jnp.where(new_ok, new, MASKED)
        top = jnp.maximum(
            jnp.max(old, axis=0, keepdims=True), jnp.max(new, axis=0, keepdims=True)
        )
        old = jnp.where(cache_ok, jnp.exp(old - top), 0.0)
        new = jnp.where(new_ok, jnp.exp(new - top), 0.0)
        total = jnp.sum(old, axis=0, keepdims=True) + jnp.sum(new, axis=0, keepdims=True)
        numer = jnp.dot(values_t[...], old.astype(BF16), preferred_element_type=F32)
        numer += lax.dot_general(new_v, new.astype(BF16), down, preferred_element_type=F32)
        num_send[to] = numer.astype(BF16)
        stat_send[to] = jnp.where(stat_row == 0, top, total)

        target = head * team + to

        @pl.when(target != me)
        def _():
            for copy in head_copies(target, to, me, plane):
                copy.start()

        @pl.when(target == me)
        def _():
            num_recv[plane] = num_send[to]
            stat_recv[plane] = stat_send[to]

        return carry

    lax.fori_loop(0, team, attend, 0)
    for at in range(team):
        source = at * team + swap(plane)

        @pl.when(source != me)
        def _():
            for copy in head_copies(me, mate, source, at):
                copy.wait_recv()

    tops = stat_recv[:, 0:1, :]
    weight = jnp.exp(tops - jnp.max(tops, axis=0, keepdims=True))
    weight = weight / jnp.sum(weight * stat_recv[:, 1:2, :], axis=0, keepdims=True)
    attention = jnp.sum(num_recv[...].astype(F32) * weight, axis=0).astype(BF16)

    n_rows = shards * rows_dev
    tile_row = lax.broadcasted_iota(jnp.int32, (n_rows // 2, LANES), 0)
    tile_lane = lax.broadcasted_iota(jnp.int32, (n_rows // 2, LANES), 1)
    parts = []
    for which in range(2 * pair):
        place = which // pair * SUB + which % pair * rows_dev
        pick = (tile_row // rows_dev == tile_lane // (2 * SUB)) & (
            tile_lane % (2 * SUB) == place + tile_row % rows_dev
        )
        pick = jnp.where(pick, 1.0, 0.0).astype(BF16)
        parts.append(
            lax.dot_general(pick, attention, across, preferred_element_type=F32).astype(BF16)
        )
    columns = jnp.concatenate(parts, axis=1)

    def spread(first, tile):
        for j in range(tile.shape[1] // LANES):
            stage[pl.ds(first + j, tile.shape[0], stride=chunks), :] = tile[
                :, j * LANES : (j + 1) * LANES
            ]

    loads[2].wait()
    weight_copy(me, sibling, 1 - core).wait_recv()
    wide = 4 * LANES
    for at in range(width // wide):
        part = wo[:, :, at * wide : (at + 1) * wide].reshape(columns.shape[1], wide)
        tile = jnp.dot(columns, part, preferred_element_type=F32)
        spread(4 * at, tile)

    half_rows = chips * rows_dev * chunks
    own_half = pl.ds(pl.multiple_of(core * half_rows, half_rows), half_rows)
    away_half = pl.ds(pl.multiple_of((1 - core) * half_rows, half_rows), half_rows)

    def others(body):
        def step_body(step, carry):
            body(lax.rem(chip + step, chips))
            return carry

        lax.fori_loop(1, chips, step_body, 0)

    def chip_copy(kind, send, recv, target_chip, source_chip):
        return remote(
            kind,
            send.at[target_chip],
            recv.at[source_chip],
            target_chip * 2 + core,
            source_chip * 2 + core,
        )

    def proj_copy(target_chip, source_chip):
        return chip_copy(PROJ, proj_send, proj_recv, target_chip, source_chip)

    def back_copy(target_chip, source_chip):
        return chip_copy(BACK, back_send, back_recv, target_chip, source_chip)

    def back_pair_copy(target, source):
        return remote(BACK_PAIR, back_away, back_near, target, source)

    proj_send[...] = stage[0:half_rows, :].astype(BF16).reshape(proj_send.shape)
    others(lambda other: proj_copy(other, chip).start())
    proj_recv[chip] = proj_send[chip]
    others(lambda other: proj_copy(chip, other).wait_recv())
    state = res_wide[...] + jnp.sum(proj_recv[...].astype(F32), axis=0)
    state = state.reshape(rows_dev, chunks, LANES)
    squares = jnp.sum(jnp.sum(state * state, axis=1, keepdims=True), axis=2, keepdims=True)
    normed = state * lax.rsqrt(squares / width + epsilon) * gain_wide[...][None]
    normed = normed.reshape(rows_dev * chunks, LANES)
    row_send[...] = normed.astype(BF16)

    def row_copy(target, source_chip):
        source = source_chip * 2 + core
        return remote(ROWS, row_send, row_recv.at[core * chips + source_chip], target, source)

    def row_pair_copy(target, source, at):
        block = row_recv.at[at]
        return pltpu.make_async_remote_copy(
            src_ref=block,
            dst_ref=block,
            send_sem=send_sem.at[ROWS_PAIR, at],
            recv_sem=recv_sem.at[ROWS_PAIR, at],
            device_id={"ctx": target},
            device_id_type=MESH,
        )

    others(lambda other: row_copy(other * 2 + core, chip).start())
    row_recv[core * chips + chip] = row_send[...]
    row_pair_copy(sibling, me, core * chips + chip).start()

    def hand_on(other):
        row_copy(me, other).wait_recv()
        row_pair_copy(sibling, me, core * chips + other).start()

    others(hand_on)

    def handed(at, carry):
        row_pair_copy(me, sibling, (1 - core) * chips + at).wait_recv()
        return carry

    lax.fori_loop(0, chips, handed, 0)
    stage[...] = row_recv[...].astype(F32).reshape(stage.shape)
    for c in range(chunks):
        x_all[:, c * LANES : (c + 1) * LANES] = stage[
            pl.ds(c, n_rows, stride=chunks), :
        ].astype(BF16)

    loads[3].wait()
    loads[4].wait()
    hidden = act.shape[1]
    step_cols = 2 * LANES if hidden % (2 * LANES) == 0 else LANES
    for at in range(hidden // step_cols):
        lanes = slice(at * step_cols, (at + 1) * step_cols)
        gate = jnp.dot(x_all[...], wg[:, lanes], preferred_element_type=F32)
        up = jnp.dot(x_all[...], wu[:, lanes], preferred_element_type=F32)
        act[:, lanes] = (gate / (1.0 + jnp.exp(-gate)) * up).astype(BF16)
    loads[5].wait()
    for at in range(width // wide):
        tile = jnp.dot(act[...], wd[:, at * wide : (at + 1) * wide], preferred_element_type=F32)
        spread(4 * at, tile * jnp.concatenate([mix[...]] * 4, axis=1))
    back_away[...] = stage[away_half, :].astype(BF16).reshape(back_away.shape)
    back_pair_copy(sibling, me).start()
    back_pair_copy(me, sibling).wait_recv()
    summed = stage[own_half, :].reshape(back_near.shape) + back_near[...].astype(F32)
    back_send[...] = summed.astype(BF16)
    others(lambda other: back_copy(other, chip).start())
    back_recv[chip] = back_send[chip]

    for step in range(1, team):
        for copy in key_copies(*near(step), mate):
            copy.wait_send()
    for at in range(team):
        target = head * team + at

        @pl.when(target != me)
        def _():
            for copy in head_copies(target, at, me, plane):
                copy.wait_send()

    peers(lambda other: q_copy(other, me).wait_send())
    weight_copy(sibling, me, core).wait_send()
    back_pair_copy(sibling, me).wait_send()

    def sent(other):
        proj_copy(other, chip).wait_send()
        row_copy(other * 2 + core, chip).wait_send()
        row_pair_copy(sibling, me, core * chips + other).wait_send()

    others(sent)
    row_pair_copy(sibling, me, core * chips + chip).wait_send()
    others(lambda other: back_copy(chip, other).wait_recv())
    final = state + jnp.sum(back_recv[...].astype(F32), axis=0).reshape(state.shape)
    for r in range(rows_dev):
        res_wide[r * chunks : (r + 1) * chunks, :] = final[r]
    for c in range(chunks):
        out_ref[:, c * LANES : (c + 1) * LANES] = res_wide[
            pl.ds(c, rows_dev, stride=chunks), :
        ]
    others(lambda other: back_copy(other, chip).wait_send())


def local(*args):
    (queries, cache_keys, _, _, _, _, residual_in, out_weight, _, expert_gate) = args[:10]
    shards = lax.axis_size("ctx")
    rows_dev, width = residual_in.shape
    capacity = max(2, 2 * rows_dev * TOP // shards)
    if not fits(shards, rows_dev, width, capacity, expert_gate.shape[0]):
        return plain(*args)
    team = shards // KV_HEADS
    hidden = expert_gate.shape[2]
    cache = cache_keys.shape[0]
    rows = rows_dev * width // LANES
    any_spec = pl.BlockSpec(memory_space=pl.ANY)
    vmem = pl.BlockSpec(memory_space=pltpu.VMEM)
    smem = pl.BlockSpec(memory_space=pltpu.SMEM)
    blocks = pltpu.VMEM((shards, rows, LANES), BF16)
    halves = pltpu.VMEM((shards // 2, rows, LANES), BF16)
    tiles = pltpu.VMEM((team, LANES, shards * SUB), BF16)
    stats = pltpu.VMEM((team, SUB, LANES), F32)
    keys = pltpu.VMEM((team, cache, LANES), BF16)
    new = pltpu.VMEM((KV_HEADS, 2 * SUB, LANES), BF16)
    flops = 2 * shards * rows_dev * width * (3 * hidden + out_weight.shape[0])
    return pl.pallas_call(
        functools.partial(layer_kernel, shards),
        out_shape=jax.ShapeDtypeStruct((rows_dev, width), F32),
        in_specs=[any_spec] * 5 + [smem] + [any_spec] * 8,
        out_specs=vmem,
        scratch_shapes=[
            pltpu.VMEM((2, *out_weight.shape), BF16),
            pltpu.VMEM((width, hidden), BF16),
            pltpu.VMEM((width, hidden), BF16),
            pltpu.VMEM((hidden, width), BF16),
            pltpu.VMEM((KV_HEADS, team * SUB, LANES), F32),
            pltpu.VMEM((KV_HEADS, team * SUB, LANES), BF16),
            pltpu.VMEM((shards, team * SUB, LANES), BF16),
            pltpu.VMEM((team, shards * SUB, LANES), BF16),
            keys,
            keys,
            pltpu.VMEM((LANES, team * cache), BF16),
            pltpu.VMEM((KV_HEADS, 2 * SUB, LANES), F32),
            new,
            new,
            tiles,
            tiles,
            stats,
            stats,
            pltpu.VMEM((shards * rows, LANES), F32),
            halves,
            halves,
            pltpu.VMEM((rows, LANES), F32),
            pltpu.VMEM((width // LANES, LANES), F32),
            pltpu.VMEM((shards, LANES), F32),
            pltpu.VMEM((shards * rows_dev, LANES), F32),
            pltpu.VMEM((rows, LANES), BF16),
            blocks,
            pltpu.VMEM((shards * rows_dev, width), BF16),
            pltpu.VMEM((shards * rows_dev, hidden), BF16),
            halves,
            halves,
            halves,
            halves,
            *(pltpu.VMEM(args[i].shape, args[i].dtype) for i in (0, 3, 4, 6)),
            pltpu.VMEM((width,), BF16),
            *(pltpu.VMEM(args[i].shape, args[i].dtype) for i in (12, 13)),
            pltpu.SemaphoreType.DMA((13,)),
            pltpu.SemaphoreType.DMA((KINDS, shards)),
            pltpu.SemaphoreType.DMA((KINDS, shards)),
        ],
        compiler_params=pltpu.CompilerParams(
            collective_id=0, has_side_effects=True, vmem_limit_bytes=60 * 1024 * 1024
        ),
        cost_estimate=pl.CostEstimate(
            flops=flops, bytes_accessed=2 * 3 * hidden * width, transcendentals=0
        ),
    )(*args).astype(BF16)


def solution(mesh):
    placed = (
        P(("groups", "ctx"), None),
        P(("groups", "ctx"), None),
        P(("groups", "ctx"), None),
        P(("groups", "ctx"), None),
        P(("groups", "ctx"), None),
        P(("groups", "ctx")),
        P(("groups", "ctx"), None),
        P("ctx", None),
        P(),
        P("ctx", None, None),
        P("ctx", None, None),
        P("ctx", None, None),
        P(("groups", "ctx"), None),
        P(("groups", "ctx"), None),
    )
    return jax.shard_map(
        local, mesh=mesh, in_specs=placed, out_specs=P(("groups", "ctx"), None), check_vma=False
    )
```
